32 devices in a mesh: rep: 2 (over x), dp: 4 (over y, core), ctx: 4 (over z).
Axes of the slice: x: 2, y: 2, z: 4, core: 2. Of those that a mesh axis runs over, the one named last changes fastest.
Arguments:
- frames: bfloat16 [8, 512, 1024], P(('rep', 'dp'), 'ctx'), may hold values from -24 to 24
- lengths: int32 [8], P(('rep', 'dp')), may hold values from 64 to 512, as said below
- cotangent: bfloat16 [8, 512, 1024], P(('rep', 'dp'), 'ctx'), may hold values from -6 to 6
- w_query: bfloat16 [1024, 512], P('dp'), may hold values from -0.5 to 0.5
- w_key: bfloat16 [1024, 512], P('dp'), may hold values from -0.5 to 0.5
- w_value: bfloat16 [1024, 512], P('dp'), may hold values from -0.1875 to 0.1875
- w_out: bfloat16 [512, 1024], P('dp'), may hold values from -0.25 to 0.25
Outputs:
- attended: bfloat16 [8, 512, 1024], P(('rep', 'dp'), 'ctx')
- grad_frames: bfloat16 [8, 512, 1024], P(('rep', 'dp'), 'ctx')
- grad_out: float32 [512, 1024], P('dp')
The draws below stay inside these ranges and needn't reach their ends.
Inputs may be any that keep to these rules, and one draw needn't show every extreme that they name: `lengths`: number of real frames of each meeting; one meeting of every draw has all 512 frames real.
All inputs are finite; a program needn't handle non-finite values.
Results may differ from the reference program's by a relative error of at most 0.025.
The reference program's roundings to bfloat16 on the way count: a program that leaves them out, or rounds other values in their place, can miss the bound.
Values may be sent and summed in bfloat16 or wider, within the bound.
A program may use at most 64 MiB of HBM per device.

```python
import jax
import jax.numpy as jnp
from jax import lax

D = 1024
HEAD = 128
HEADS = 4
HD = 512
FRAMES = 512
MEETINGS = 8


def draw_frames(key, part):
    normal_key = jax.random.fold_in(key, 0)
    base = jax.random.normal(normal_key, (MEETINGS, FRAMES, D), jnp.float32)
    return jnp.clip(base, -6.0, 6.0).astype(jnp.bfloat16)


def draw_lengths(key, part):
    first_key, second_key, pick_key = jax.random.split(key, 3)
    lowest = FRAMES // 8
    first_draw = jax.random.randint(first_key, (MEETINGS,), 0, FRAMES - lowest + 1)
    second_draw = jax.random.randint(second_key, (MEETINGS,), 0, FRAMES - lowest + 1)
    chosen = jax.random.randint(pick_key, (), 0, MEETINGS)
    base = lowest + jnp.minimum(first_draw, second_draw)
    return jnp.where(jnp.arange(MEETINGS) == chosen, FRAMES, base).astype(jnp.int32)


def block_levels(rng, extent, shards, smallest, top_value):
    gain = 1.0
    for axis_at, shards_of in shards:
        steps = jax.random.uniform(jax.random.fold_in(jax.random.fold_in(rng, 6), axis_at), (shards_of,), jnp.float32, smallest / len(shards), top_value / len(shards))
        gain = gain * jnp.repeat(jnp.exp(steps), extent[axis_at] // shards_of).reshape((-1,) + (1,) * (len(extent) - 1 - axis_at))
    return gain


def centred(key, dims, spread, most, cuts=(), held_as=jnp.bfloat16):
    values = jax.random.normal(key, dims, jnp.float32) * spread
    if len(cuts) > 0:
        values = block_levels(key, dims, cuts, -0.22, 0.18) * values
    return jnp.clip(values, min=-most, max=most).astype(held_as)


def setup_inputs(seed: int = 0) -> dict:
    arg_keys = jax.random.split(jax.random.key(seed), 8)
    return {
        "frames": draw_frames(jax.random.fold_in(arg_keys[7], 71), 0),
        "lengths": draw_lengths(jax.random.fold_in(arg_keys[7], 71), 0),
        "cotangent": centred(arg_keys[2], (MEETINGS, FRAMES, D), 1.0, 6.0, ((0, 8), (1, 4))),
        "w_query": centred(arg_keys[3], (D, HD), (D ** -0.5), 0.5, ((0, 4),)),
        "w_key": centred(arg_keys[4], (D, HD), (D ** -0.5), 0.5, ((0, 4),)),
        "w_value": centred(arg_keys[5], (D, HD), D ** -0.5, 0.1875, ((0, 4),)),
        "w_out": centred(arg_keys[6], (HD, D), HD ** -0.5, 0.25, ((0, 4),)),
    }


MASKED_SCORE = -1.0e30


def meeting_pass(inputs, upstream, length, w_query, w_key, w_value, w_out):
    frame_count = inputs.shape[0]
    score_scale = HEAD ** -0.5
    usable = jnp.arange(frame_count) < length
    queries = jnp.dot(inputs, w_query, preferred_element_type=jnp.float32).astype(jnp.bfloat16)
    keys = jnp.dot(inputs, w_key, preferred_element_type=jnp.float32).astype(jnp.bfloat16)
    values = jnp.dot(inputs, w_value, preferred_element_type=jnp.float32).astype(jnp.bfloat16)
    masked_grad = jnp.where(usable[:, None], upstream, jnp.zeros_like(upstream))
    contexts = []
    logsums = []
    for head in range(HEADS):
        columns = slice(head * HEAD, (head + 1) * HEAD)
        scores = jnp.dot(queries[:, columns], keys[:, columns].T, preferred_element_type=jnp.float32) * score_scale
        scores = jnp.where(usable[None, :], scores, MASKED_SCORE)
        maxima = jnp.max(scores, axis=1)
        exponent = jnp.where(usable[None, :], jnp.exp(scores - maxima[:, None]), 0.0)
        totals = jnp.sum(exponent, axis=1)
        mixed = jnp.dot(exponent.astype(jnp.bfloat16), values[:, columns], preferred_element_type=jnp.float32)
        contexts.append(mixed / totals[:, None])
        logsums.append(maxima + jnp.log(totals))
    context = jnp.concatenate(contexts, axis=1).astype(jnp.bfloat16)
    attended = jnp.dot(context, w_out, preferred_element_type=jnp.float32)
    attended = jnp.where(usable[:, None], attended, 0.0).astype(jnp.bfloat16)
    grad_term = jnp.dot(context.T, masked_grad, preferred_element_type=jnp.float32)
    grad_context = jnp.dot(masked_grad, w_out.T, preferred_element_type=jnp.float32).astype(jnp.bfloat16)
    grad_queries = []
    grad_keys = []
    grad_values = []
    for head in range(HEADS):
        columns = slice(head * HEAD, (head + 1) * HEAD)
        deltas = jnp.sum(grad_context[:, columns].astype(jnp.float32) * context[:, columns].astype(jnp.float32), axis=1)
        scores = jnp.dot(queries[:, columns], keys[:, columns].T, preferred_element_type=jnp.float32) * score_scale
        attention = jnp.where(usable[None, :], jnp.exp(scores - logsums[head][:, None]), 0.0)
        grad_values.append(jnp.dot(attention.astype(jnp.bfloat16).T, grad_context[:, columns], preferred_element_type=jnp.float32))
        grad_prob = jnp.dot(grad_context[:, columns], values[:, columns].T, preferred_element_type=jnp.float32)
        grad_score = (attention * (grad_prob - deltas[:, None])).astype(jnp.bfloat16)
        grad_queries.append(jnp.dot(grad_score, keys[:, columns], preferred_element_type=jnp.float32) * score_scale)
        grad_keys.append(jnp.dot(grad_score.T, queries[:, columns], preferred_element_type=jnp.float32) * score_scale)
    grad_query = jnp.concatenate(grad_queries, axis=1).astype(jnp.bfloat16)
    grad_key = jnp.concatenate(grad_keys, axis=1).astype(jnp.bfloat16)
    grad_value = jnp.concatenate(grad_values, axis=1).astype(jnp.bfloat16)
    grad_input = jnp.dot(grad_query, w_query.T, preferred_element_type=jnp.float32)
    grad_input = grad_input + jnp.dot(grad_key, w_key.T, preferred_element_type=jnp.float32)
    grad_input = grad_input + jnp.dot(grad_value, w_value.T, preferred_element_type=jnp.float32)
    return attended, grad_input.astype(jnp.bfloat16), grad_term


def reference(frames, lengths, cotangent, w_query, w_key, w_value, w_out):
    def one_meeting(meeting):
        return meeting_pass(meeting[0], meeting[1], meeting[2], w_query, w_key, w_value, w_out)

    attended, grad_frames, grad_terms = lax.map(one_meeting, (frames, cotangent, lengths))
    return attended, grad_frames, jnp.sum(grad_terms, axis=0)
```

```python
import functools
import math

import jax
import jax.numpy as jnp
from jax import lax
from jax.experimental import pallas as pl
from jax.experimental.pallas import tpu as pltpu
from jax.sharding import PartitionSpec as P

HEAD = 128


MASKED_SCORE = -1e30


def head_split(matrix, head_count):
    return matrix.reshape(matrix.shape[0], head_count, matrix.shape[1] // head_count)


def forward_step(carry, key_part, value_part, offset, query_heads, length, score_scale):
    head_count = query_heads.shape[1]
    amount = key_part.shape[0]
    maxima, totals, accumulated = carry
    key_heads = head_split(key_part, head_count)
    value_heads = head_split(value_part, head_count)
    scores = (
        jnp.einsum("rhe,nhe->hrn", query_heads, key_heads, preferred_element_type=jnp.float32)
        * score_scale
    )
    usable = offset + jnp.arange(amount) < length
    scores = jnp.where(usable[None, None, :], scores, MASKED_SCORE)
    new_maxima = jnp.maximum(maxima, jnp.max(scores, axis=2))
    factor = jnp.exp(maxima - new_maxima)
    exponent = jnp.where(usable[None, None, :], jnp.exp(scores - new_maxima[:, :, None]), 0.0)
    totals = totals * factor + jnp.sum(exponent, axis=2)
    mixed = jnp.einsum(
        "hrn,nhe->hre",
        exponent.astype(jnp.bfloat16),
        value_heads,
        preferred_element_type=jnp.float32,
    )
    accumulated = accumulated * factor[:, :, None] + mixed
    return (new_maxima, totals, accumulated)


def query_step(
    grad_accum,
    key_part,
    value_part,
    offset,
    query_heads,
    context_heads,
    logsum,
    deltas,
    length,
    score_scale,
):
    head_count = query_heads.shape[1]
    amount = key_part.shape[0]
    key_heads = head_split(key_part, head_count)
    value_heads = head_split(value_part, head_count)
    scores = (
        jnp.einsum("rhe,nhe->hrn", query_heads, key_heads, preferred_element_type=jnp.float32)
        * score_scale
    )
    usable = offset + jnp.arange(amount) < length
    attention = jnp.where(usable[None, None, :], jnp.exp(scores - logsum[:, :, None]), 0.0)
    grad_prob = jnp.einsum(
        "rhe,nhe->hrn", context_heads, value_heads, preferred_element_type=jnp.float32
    )
    grad_score = (attention * (grad_prob - deltas[:, :, None])).astype(jnp.bfloat16)
    added = jnp.einsum("hrn,nhe->rhe", grad_score, key_heads, preferred_element_type=jnp.float32)
    return grad_accum + added * score_scale


def key_step(
    query_part,
    context_part,
    all_logsum,
    all_deltas,
    key_heads,
    value_heads,
    key_usable,
    score_scale,
):
    head_count = key_heads.shape[1]
    query_heads = head_split(query_part, head_count)
    context_heads = head_split(context_part, head_count)
    scores = (
        jnp.einsum("rhe,nhe->hrn", query_heads, key_heads, preferred_element_type=jnp.float32)
        * score_scale
    )
    attention = jnp.where(key_usable[None, None, :], jnp.exp(scores - all_logsum[:, :, None]), 0.0)
    grad_value = jnp.einsum(
        "hrn,rhe->nhe",
        attention.astype(jnp.bfloat16),
        context_heads,
        preferred_element_type=jnp.float32,
    )
    grad_prob = jnp.einsum(
        "rhe,nhe->hrn", context_heads, value_heads, preferred_element_type=jnp.float32
    )
    grad_score = (attention * (grad_prob - all_deltas[:, :, None])).astype(jnp.bfloat16)
    added = jnp.einsum("hrn,rhe->nhe", grad_score, query_heads, preferred_element_type=jnp.float32)
    return (added * score_scale, grad_value)


def back_project(gradient, weight):
    return lax.dot_general(
        gradient, weight, (((1,), (1,)), ((), ())), preferred_element_type=jnp.float32
    )


def shards(frames, lengths, cotangent, w_query, w_key, w_value, w_out):
    full_query, full_key, full_value, full_out = (
        lax.all_gather(w_query, "dp", axis=0, tiled=True),
        lax.all_gather(w_key, "dp", axis=0, tiled=True),
        lax.all_gather(w_value, "dp", axis=0, tiled=True),
        lax.all_gather(w_out, "dp", axis=0, tiled=True),
    )
    inputs = frames[0]
    upstream = cotangent[0]
    length = lengths[0]
    row_count = inputs.shape[0]
    inner_width = full_query.shape[1]
    head_count = inner_width // HEAD
    score_scale = HEAD ** (-0.5)
    first_frame = lax.axis_index("ctx") * row_count
    row_usable = first_frame + jnp.arange(row_count) < length
    queries = jnp.dot(inputs, full_query, preferred_element_type=jnp.float32).astype(jnp.bfloat16)
    keys = jnp.dot(inputs, full_key, preferred_element_type=jnp.float32).astype(jnp.bfloat16)
    values = jnp.dot(inputs, full_value, preferred_element_type=jnp.float32).astype(jnp.bfloat16)
    query_heads = head_split(queries, head_count)
    key_heads = head_split(keys, head_count)
    value_heads = head_split(values, head_count)
    start_state = (
        jnp.full((head_count, row_count), MASKED_SCORE, jnp.float32),
        jnp.zeros((head_count, row_count), jnp.float32),
        jnp.zeros((head_count, row_count, HEAD), jnp.float32),
    )
    all_keys, all_values = (
        lax.all_gather(keys, "ctx", axis=0, tiled=True),
        lax.all_gather(values, "ctx", axis=0, tiled=True),
    )
    key_block = row_count * math.gcd(max(1, 512 // row_count), lax.axis_size("ctx"))
    block_count = all_keys.shape[0] // key_block
    key_blocks = all_keys.reshape(block_count, key_block, inner_width)
    value_blocks = all_values.reshape(block_count, key_block, inner_width)
    block_starts = jnp.arange(block_count, dtype=jnp.int32) * key_block

    def scan_forward(current, scan_item):
        return (
            forward_step(
                current, scan_item[0], scan_item[1], scan_item[2], query_heads, length, score_scale
            ),
            None,
        )

    softmax_state, unused = lax.scan(
        scan_forward, start_state, (key_blocks, value_blocks, block_starts)
    )
    maxima, totals, accumulated = softmax_state
    context = (
        (accumulated / totals[:, :, None])
        .transpose(1, 0, 2)
        .reshape(row_count, inner_width)
        .astype(jnp.bfloat16)
    )
    logsum = maxima + jnp.log(totals)
    attended = jnp.dot(context, full_out, preferred_element_type=jnp.float32)
    attended = jnp.where(row_usable[:, None], attended, 0.0).astype(jnp.bfloat16)
    masked_grad = jnp.where(row_usable[:, None], upstream, jnp.zeros_like(upstream))
    grad_context = back_project(masked_grad, full_out).astype(jnp.bfloat16)
    deltas = jnp.sum(
        (grad_context.astype(jnp.float32) * context.astype(jnp.float32)).reshape(
            row_count, head_count, HEAD
        ),
        axis=2,
    )
    context_heads = head_split(grad_context, head_count)
    delta_heads = deltas.T
    all_logsum, all_deltas = (
        lax.all_gather(logsum, "ctx", axis=1, tiled=True),
        lax.all_gather(delta_heads, "ctx", axis=1, tiled=True),
    )
    zero_grad = jnp.zeros((row_count, head_count, HEAD), jnp.float32)

    def scan_query(current, scan_item):
        return (
            query_step(
                current,
                scan_item[0],
                scan_item[1],
                scan_item[2],
                query_heads,
                context_heads,
                logsum,
                delta_heads,
                length,
                score_scale,
            ),
            None,
        )

    grad_query, unused = lax.scan(scan_query, zero_grad, (key_blocks, value_blocks, block_starts))
    grad_key, grad_value = key_step(
        lax.all_gather(queries, "ctx", axis=0, tiled=True),
        lax.all_gather(grad_context, "ctx", axis=0, tiled=True),
        all_logsum,
        all_deltas,
        key_heads,
        value_heads,
        row_usable,
        score_scale,
    )
    grad_query = grad_query.reshape(row_count, inner_width).astype(jnp.bfloat16)
    grad_key = grad_key.reshape(row_count, inner_width).astype(jnp.bfloat16)
    grad_value = grad_value.reshape(row_count, inner_width).astype(jnp.bfloat16)
    grad_input = (
        back_project(grad_query, full_query)
        + back_project(grad_key, full_key)
        + back_project(grad_value, full_value)
    )
    grad_frames = grad_input.astype(jnp.bfloat16)
    summed_grad = lax.psum(
        lax.dot_general(
            context, masked_grad, (((0,), (0,)), ((), ())), preferred_element_type=jnp.float32
        ),
        ("rep", "ctx"),
    )
    grad_out = lax.psum_scatter(summed_grad, "dp", scatter_dimension=0, tiled=True)
    return (attended[None], grad_frames[None], grad_out)


MESH = pl.DeviceIdType.MESH


def dot(left, right, left_dim, right_dim):
    return lax.dot_general(
        left, right, (((left_dim,), (right_dim,)), ((), ())), preferred_element_type=jnp.float32
    )


def fused_kernel(
    frames_ref,
    length_ref,
    cot_ref,
    wq_ref,
    wk_ref,
    wv_ref,
    wo_ref,
    attended_ref,
    grad_frames_ref,
    grad_out_ref,
    xs,
    cs,
    wq,
    wk,
    wv,
    wo,
    qs,
    ks,
    vs,
    gs,
    ctx,
    logsum,
    deltas,
    dq,
    dk,
    dv,
    part,
    part_in,
    slices,
    send_sem,
    recv_sem,
):
    rep, dp, z = lax.axis_index("rep"), lax.axis_index("dp"), lax.axis_index("ctx")
    count = 4
    heads = 4
    rows = frames_ref.shape[1]
    full = rows * count
    width = slices.shape[2]
    scale = HEAD ** (-0.5)
    sibling = dp + 1 - 2 * lax.rem(dp, 2)
    across = lax.rem(dp + 2, 4)
    across_sibling = lax.rem(sibling + 2, 4)
    other_rep = 1 - rep
    group = rep * 4 + dp

    barrier = pltpu.get_barrier_semaphore()
    for step in range(1, count):
        pl.semaphore_signal(
            barrier, inc=1, device_id=(rep, dp, lax.rem(z + step, count)), device_id_type=MESH
        )
    for step in range(1, 8):
        peer = lax.rem(group + step, 8)
        pl.semaphore_signal(
            barrier, inc=1, device_id=(peer // 4, lax.rem(peer, 4), z), device_id_type=MESH
        )
    pl.semaphore_wait(barrier, 10)

    def remote(source, target, index, device):
        return pltpu.make_async_remote_copy(
            src_ref=source,
            dst_ref=target,
            send_sem=send_sem.at[index],
            recv_sem=recv_sem.at[index],
            device_id=device,
            device_id_type=MESH,
        )

    def chain(which, side, hop):
        sign = 1 - 2 * side
        home, pool = ((frames_ref, xs), (cot_ref, cs))[which]
        owner = z - sign * (hop - 1)
        source = home.at[0] if hop == 1 else pool.at[jnp.clip(owner, 0, count - 1)]
        slot = jnp.clip(owner, 0, count - 1)
        target = jnp.clip(z + sign, 0, count - 1)
        index = which * 6 + side * 3 + hop - 1
        valid = (z + sign >= 0) & (z + sign < count) & (owner >= 0) & (owner < count)
        return valid, remote(source, pool.at[slot], index, (rep, dp, target))

    def chain_send(which, hop):
        for side in range(2):
            valid, copy = chain(which, side, hop)

            @pl.when(valid)
            def _():
                copy.start()

    def chain_recv(which, hop):
        for side in range(2):
            sign = 1 - 2 * side
            pool = (xs, cs)[which]
            owner = z - sign * hop
            slot = jnp.clip(owner, 0, count - 1)
            index = which * 6 + side * 3 + hop - 1

            @pl.when((owner >= 0) & (owner < count))
            def _():
                remote(pool.at[slot], pool.at[slot], index, (rep, dp, z)).wait_recv()

    weights = ((wk_ref, wk), (wv_ref, wv), (wq_ref, wq), (wo_ref, wo))

    def half(ref, which):
        size = ref.shape[0] // 2
        return ref.at[pl.ds(pl.multiple_of(which * size, size), size)]

    def weight_copy(piece, step):
        shard, pool = weights[piece]
        index = 12 + piece * 5 + step
        if step == 0:
            return remote(shard, pool.at[dp], index, (rep, sibling, z))
        if step == 1:
            return remote(half(shard, rep), half(pool.at[dp], rep), index, (rep, across, z))
        mine = pool.at[across]
        if step == 2:
            return remote(half(mine, rep), half(mine, rep), index, (rep, sibling, z))
        if step == 3:
            return remote(half(mine, rep), half(mine, rep), index, (other_rep, dp, z))
        return remote(half(mine, other_rep), half(mine, other_rep), index, (rep, sibling, z))

    def weight_recv(piece, step):
        pool = weights[piece][1]
        index = 12 + piece * 5 + step
        if step == 0:
            target = pool.at[sibling]
        elif step == 1:
            target = half(pool.at[across], rep)
        elif step == 2:
            target = half(pool.at[across_sibling], rep)
        elif step == 3:
            target = half(pool.at[across], other_rep)
        else:
            target = half(pool.at[across_sibling], other_rep)
        remote(target, target, index, (rep, dp, z)).wait_recv()

    chain_send(0, 1)
    for piece in range(4):
        weight_copy(piece, 1).start()
    for piece in range(4):
        weight_copy(piece, 0).start()
    for shard, pool in weights:
        pool[dp] = shard[...]
    xs[z] = frames_ref[0]
    cs[z] = cot_ref[0]

    def pass_weights(piece):
        weight_recv(piece, 1)
        weight_copy(piece, 3).start()
        weight_copy(piece, 2).start()

    def finish_weights(piece):
        weight_recv(piece, 3)
        weight_copy(piece, 4).start()

    pass_weights(0)
    chain_recv(0, 1)
    chain_send(0, 2)
    chain_send(1, 1)
    pass_weights(1)
    finish_weights(0)
    pass_weights(2)
    finish_weights(1)
    chain_recv(0, 2)
    chain_send(0, 3)
    pass_weights(3)
    finish_weights(2)
    finish_weights(3)
    for piece in range(4):
        for step in (0, 2, 4):
            weight_recv(piece, step)
    chain_recv(1, 1)
    chain_send(1, 2)
    chain_recv(0, 3)

    length = length_ref[0]

    def project(block, carry):
        inputs = xs[block]
        start = pl.multiple_of(block * rows, rows)
        for pool, kept in ((wk, ks), (wv, vs), (wq, qs)):
            matrix = dot(inputs, pool[...].reshape(1024, 512), 1, 0).astype(jnp.bfloat16)
            for head in range(heads):
                kept[head, pl.ds(start, rows), :] = matrix[:, head * HEAD : (head + 1) * HEAD]
        return carry

    lax.fori_loop(0, count, project, 0)

    def key_mask(amount):
        return lax.broadcasted_iota(jnp.int32, (amount, full), 1) < length

    def forward(step, carry):
        head = step // 2
        amount = full // 2
        start = pl.multiple_of(lax.rem(step, 2) * amount, amount)
        usable = key_mask(amount)
        scores = dot(qs[head, pl.ds(start, amount), :], ks[head], 1, 1) * scale
        scores = jnp.where(usable, scores, MASKED_SCORE)
        maxima = jnp.max(scores, axis=1, keepdims=True)
        exponent = jnp.where(usable, jnp.exp(scores - maxima), 0.0)
        totals = jnp.sum(exponent, axis=1, keepdims=True)
        mixed = dot(exponent.astype(jnp.bfloat16), vs[head], 1, 0)
        ctx[head, pl.ds(start, amount), :] = (mixed / totals).astype(jnp.bfloat16)
        logsum[head, pl.ds(start, amount), :] = maxima + jnp.log(totals)
        return carry

    lax.fori_loop(0, 4, forward, 0)
    chain_recv(1, 2)
    chain_send(1, 3)
    lax.fori_loop(4, 8, forward, 0)

    own = pl.ds(pl.multiple_of(z * rows, rows), rows)
    own_context = jnp.concatenate([ctx[head, own, :] for head in range(heads)], axis=1)
    attended = dot(own_context, wo[...].reshape(512, 1024), 1, 0)
    row_at = z * rows + lax.broadcasted_iota(jnp.int32, attended.shape, 0)
    attended_ref[0] = jnp.where(row_at < length, attended, 0.0).astype(jnp.bfloat16)

    chain_recv(1, 3)
    for which in range(2):
        for hop in range(1, count):
            for side in range(2):
                valid, copy = chain(which, side, hop)

                @pl.when(valid)
                def _():
                    copy.wait_send()

    def context_gradient(block, carry):
        start = pl.multiple_of(block * rows, rows)
        upstream = cs[block].astype(jnp.float32)
        at = start + lax.broadcasted_iota(jnp.int32, upstream.shape, 0)
        masked = jnp.where(at < length, upstream, 0.0).astype(jnp.bfloat16)
        cs[block] = masked
        matrix = dot(masked, wo[...].reshape(512, 1024), 1, 1).astype(jnp.bfloat16)
        for head in range(heads):
            piece = matrix[:, head * HEAD : (head + 1) * HEAD]
            gs[head, pl.ds(start, rows), :] = piece
            terms = piece.astype(jnp.float32) * ctx[head, pl.ds(start, rows), :].astype(jnp.float32)
            deltas[head, pl.ds(start, rows), :] = jnp.sum(terms, axis=1, keepdims=True)
        return carry

    lax.fori_loop(0, count, context_gradient, 0)

    columns = pl.ds(pl.multiple_of(z * width, width), width)
    masked_slice = cs[:, :, columns].reshape(full, width)
    for head in range(heads):
        part[head] = dot(ctx[head], masked_slice, 0, 0).astype(jnp.bfloat16)

    def part_copy(step):
        peer = lax.rem(group + step, 8)
        peer_dp = lax.rem(peer, 4)
        return remote(part.at[peer_dp], part_in.at[step], 32 + step, (peer // 4, peer_dp, z))

    for step in range(1, 8):
        part_copy(step).start()

    def backward(head, carry):
        queries, keys, values, grads = qs[head], ks[head], vs[head], gs[head]
        own_keys, own_values = ks[head, own, :], vs[head, own, :]
        scores = dot(queries, own_keys, 1, 1) * scale
        at = z * rows + lax.broadcasted_iota(jnp.int32, scores.shape, 1)
        attention = jnp.where(at < length, jnp.exp(scores - logsum[head]), 0.0)
        dv[head] = dot(attention.astype(jnp.bfloat16), grads, 0, 0).astype(jnp.bfloat16)
        grad_prob = dot(grads, own_values, 1, 1)
        grad_score = (attention * (grad_prob - deltas[head])).astype(jnp.bfloat16)
        dk[head] = (dot(grad_score, queries, 0, 0) * scale).astype(jnp.bfloat16)
        scores = dot(qs[head, own, :], keys, 1, 1) * scale
        attention = jnp.where(key_mask(rows), jnp.exp(scores - logsum[head, own, :]), 0.0)
        grad_prob = dot(gs[head, own, :], values, 1, 1)
        grad_score = (attention * (grad_prob - deltas[head, own, :])).astype(jnp.bfloat16)
        dq[head] = (dot(grad_score, keys, 1, 0) * scale).astype(jnp.bfloat16)
        return carry

    lax.fori_loop(0, heads, backward, 0)

    total = part[dp].astype(jnp.float32)
    for step in range(1, 8):
        part_copy(step).wait_recv()
        total = total + part_in[step].astype(jnp.float32)
    slices[z] = total.astype(jnp.bfloat16)

    def slice_copy(step):
        return remote(
            slices.at[z], slices.at[z], 40 + step, (rep, dp, lax.rem(z + step, count))
        )

    for step in range(1, count):
        slice_copy(step).start()

    grads = [
        jnp.concatenate([kept[head] for head in range(heads)], axis=1) for kept in (dq, dk, dv)
    ]
    for shard in range(4):
        added = (
            dot(grads[0], wq[shard], 1, 1)
            + dot(grads[1], wk[shard], 1, 1)
            + dot(grads[2], wv[shard], 1, 1)
        )
        grad_frames_ref[0, :, shard * 256 : (shard + 1) * 256] = added.astype(jnp.bfloat16)

    for piece in range(4):
        for step in range(5):
            weight_copy(piece, step).wait_send()
    for step in range(1, 8):
        part_copy(step).wait_send()
    for step in range(1, count):
        source = lax.rem(z + count - step, count)
        remote(slices.at[source], slices.at[source], 40 + step, (rep, dp, z)).wait_recv()
    for step in range(1, count):
        slice_copy(step).wait_send()
    for at in range(count):
        grad_out_ref[:, at * width : (at + 1) * width] = slices[at].astype(jnp.float32)


def fused(frames, lengths, cotangent, w_query, w_key, w_value, w_out):
    vmem = pl.BlockSpec(memory_space=pltpu.VMEM)
    bf16, f32 = jnp.bfloat16, jnp.float32
    per_head = pltpu.VMEM((4, 512, HEAD), bf16)
    own_head = pltpu.VMEM((4, 128, HEAD), bf16)
    return pl.pallas_call(
        fused_kernel,
        out_shape=(
            jax.ShapeDtypeStruct(frames.shape, bf16),
            jax.ShapeDtypeStruct(frames.shape, bf16),
            jax.ShapeDtypeStruct(w_out.shape, f32),
        ),
        in_specs=[vmem, pl.BlockSpec(memory_space=pltpu.SMEM)] + [vmem] * 5,
        out_specs=(vmem, vmem, vmem),
        scratch_shapes=[
            pltpu.VMEM((4, 128, 1024), bf16),
            pltpu.VMEM((4, 128, 1024), bf16),
            pltpu.VMEM((4, 256, 512), bf16),
            pltpu.VMEM((4, 256, 512), bf16),
            pltpu.VMEM((4, 256, 512), bf16),
            pltpu.VMEM((4, 128, 1024), bf16),
            per_head,
            per_head,
            per_head,
            per_head,
            per_head,
            pltpu.VMEM((4, 512, 1), f32),
            pltpu.VMEM((4, 512, 1), f32),
            own_head,
            own_head,
            own_head,
            pltpu.VMEM((4, 128, 256), bf16),
            pltpu.VMEM((8, 128, 256), bf16),
            pltpu.VMEM((4, 128, 256), bf16),
            pltpu.SemaphoreType.DMA((44,)),
            pltpu.SemaphoreType.DMA((44,)),
        ],
        compiler_params=pltpu.CompilerParams(
            collective_id=0, has_side_effects=True, vmem_limit_bytes=48 * 1024 * 1024
        ),
    )(frames, lengths, cotangent, w_query, w_key, w_value, w_out)


def either(sizes, frames, lengths, cotangent, w_query, w_key, w_value, w_out):
    fits = sizes == (2, 4, 4) and frames.shape == (1, 128, 1024) and w_query.shape == (256, 512)
    chosen = fused if fits else shards
    return chosen(frames, lengths, cotangent, w_query, w_key, w_value, w_out)


def solution(mesh):
    in_specs = (
        P(("rep", "dp"), "ctx", None),
        P(("rep", "dp")),
        P(("rep", "dp"), "ctx", None),
        P("dp", None),
        P("dp", None),
        P("dp", None),
        P("dp", None),
    )
    out_specs = (P(("rep", "dp"), "ctx", None), P(("rep", "dp"), "ctx", None), P("dp", None))
    sizes = (mesh.shape["rep"], mesh.shape["dp"], mesh.shape["ctx"])
    body = functools.partial(either, sizes)
    return jax.shard_map(body, mesh=mesh, in_specs=in_specs, out_specs=out_specs, check_vma=False)
```

```python
import functools
import math

import jax
import jax.numpy as jnp
from jax import lax
from jax.experimental import pallas as pl
from jax.experimental.pallas import tpu as pltpu
from jax.sharding import PartitionSpec as P

HEAD = 128


MASKED_SCORE = -1e30


def head_split(matrix, head_count):
    return matrix.reshape(matrix.shape[0], head_count, matrix.shape[1] // head_count)


def forward_step(carry, key_part, value_part, offset, query_heads, length, score_scale):
    head_count = query_heads.shape[1]
    amount = key_part.shape[0]
    maxima, totals, accumulated = carry
    key_heads = head_split(key_part, head_count)
    value_heads = head_split(value_part, head_count)
    scores = (
        jnp.einsum("rhe,nhe->hrn", query_heads, key_heads, preferred_element_type=jnp.float32)
        * score_scale
    )
    usable = offset + jnp.arange(amount) < length
    scores = jnp.where(usable[None, None, :], scores, MASKED_SCORE)
    new_maxima = jnp.maximum(maxima, jnp.max(scores, axis=2))
    factor = jnp.exp(maxima - new_maxima)
    exponent = jnp.where(usable[None, None, :], jnp.exp(scores - new_maxima[:, :, None]), 0.0)
    totals = totals * factor + jnp.sum(exponent, axis=2)
    mixed = jnp.einsum(
        "hrn,nhe->hre",
        exponent.astype(jnp.bfloat16),
        value_heads,
        preferred_element_type=jnp.float32,
    )
    accumulated = accumulated * factor[:, :, None] + mixed
    return (new_maxima, totals, accumulated)


def query_step(
    grad_accum,
    key_part,
    value_part,
    offset,
    query_heads,
    context_heads,
    logsum,
    deltas,
    length,
    score_scale,
):
    head_count = query_heads.shape[1]
    amount = key_part.shape[0]
    key_heads = head_split(key_part, head_count)
    value_heads = head_split(value_part, head_count)
    scores = (
        jnp.einsum("rhe,nhe->hrn", query_heads, key_heads, preferred_element_type=jnp.float32)
        * score_scale
    )
    usable = offset + jnp.arange(amount) < length
    attention = jnp.where(usable[None, None, :], jnp.exp(scores - logsum[:, :, None]), 0.0)
    grad_prob = jnp.einsum(
        "rhe,nhe->hrn", context_heads, value_heads, preferred_element_type=jnp.float32
    )
    grad_score = (attention * (grad_prob - deltas[:, :, None])).astype(jnp.bfloat16)
    added = jnp.einsum("hrn,nhe->rhe", grad_score, key_heads, preferred_element_type=jnp.float32)
    return grad_accum + added * score_scale


def key_step(
    query_part,
    context_part,
    all_logsum,
    all_deltas,
    key_heads,
    value_heads,
    key_usable,
    score_scale,
):
    head_count = key_heads.shape[1]
    query_heads = head_split(query_part, head_count)
    context_heads = head_split(context_part, head_count)
    scores = (
        jnp.einsum("rhe,nhe->hrn", query_heads, key_heads, preferred_element_type=jnp.float32)
        * score_scale
    )
    attention = jnp.where(key_usable[None, None, :], jnp.exp(scores - all_logsum[:, :, None]), 0.0)
    grad_value = jnp.einsum(
        "hrn,rhe->nhe",
        attention.astype(jnp.bfloat16),
        context_heads,
        preferred_element_type=jnp.float32,
    )
    grad_prob = jnp.einsum(
        "rhe,nhe->hrn", context_heads, value_heads, preferred_element_type=jnp.float32
    )
    grad_score = (attention * (grad_prob - all_deltas[:, :, None])).astype(jnp.bfloat16)
    added = jnp.einsum("hrn,rhe->nhe", grad_score, query_heads, preferred_element_type=jnp.float32)
    return (added * score_scale, grad_value)


def back_project(gradient, weight):
    return lax.dot_general(
        gradient, weight, (((1,), (1,)), ((), ())), preferred_element_type=jnp.float32
    )


def shards(frames, lengths, cotangent, w_query, w_key, w_value, w_out):
    full_query, full_key, full_value, full_out = (
        lax.all_gather(w_query, "dp", axis=0, tiled=True),
        lax.all_gather(w_key, "dp", axis=0, tiled=True),
        lax.all_gather(w_value, "dp", axis=0, tiled=True),
        lax.all_gather(w_out, "dp", axis=0, tiled=True),
    )
    inputs = frames[0]
    upstream = cotangent[0]
    length = lengths[0]
    row_count = inputs.shape[0]
    inner_width = full_query.shape[1]
    head_count = inner_width // HEAD
    score_scale = HEAD ** (-0.5)
    first_frame = lax.axis_index("ctx") * row_count
    row_usable = first_frame + jnp.arange(row_count) < length
    queries = jnp.dot(inputs, full_query, preferred_element_type=jnp.float32).astype(jnp.bfloat16)
    keys = jnp.dot(inputs, full_key, preferred_element_type=jnp.float32).astype(jnp.bfloat16)
    values = jnp.dot(inputs, full_value, preferred_element_type=jnp.float32).astype(jnp.bfloat16)
    query_heads = head_split(queries, head_count)
    key_heads = head_split(keys, head_count)
    value_heads = head_split(values, head_count)
    start_state = (
        jnp.full((head_count, row_count), MASKED_SCORE, jnp.float32),
        jnp.zeros((head_count, row_count), jnp.float32),
        jnp.zeros((head_count, row_count, HEAD), jnp.float32),
    )
    all_keys, all_values = (
        lax.all_gather(keys, "ctx", axis=0, tiled=True),
        lax.all_gather(values, "ctx", axis=0, tiled=True),
    )
    key_block = row_count * math.gcd(max(1, 512 // row_count), lax.axis_size("ctx"))
    block_count = all_keys.shape[0] // key_block
    key_blocks = all_keys.reshape(block_count, key_block, inner_width)
    value_blocks = all_values.reshape(block_count, key_block, inner_width)
    block_starts = jnp.arange(block_count, dtype=jnp.int32) * key_block

    def scan_forward(current, scan_item):
        return (
            forward_step(
                current, scan_item[0], scan_item[1], scan_item[2], query_heads, length, score_scale
            ),
            None,
        )

    softmax_state, unused = lax.scan(
        scan_forward, start_state, (key_blocks, value_blocks, block_starts)
    )
    maxima, totals, accumulated = softmax_state
    context = (
        (accumulated / totals[:, :, None])
        .transpose(1, 0, 2)
        .reshape(row_count, inner_width)
        .astype(jnp.bfloat16)
    )
    logsum = maxima + jnp.log(totals)
    attended = jnp.dot(context, full_out, preferred_element_type=jnp.float32)
    attended = jnp.where(row_usable[:, None], attended, 0.0).astype(jnp.bfloat16)
    masked_grad = jnp.where(row_usable[:, None], upstream, jnp.zeros_like(upstream))
    grad_context = back_project(masked_grad, full_out).astype(jnp.bfloat16)
    deltas = jnp.sum(
        (grad_context.astype(jnp.float32) * context.astype(jnp.float32)).reshape(
            row_count, head_count, HEAD
        ),
        axis=2,
    )
    context_heads = head_split(grad_context, head_count)
    delta_heads = deltas.T
    all_logsum, all_deltas = (
        lax.all_gather(logsum, "ctx", axis=1, tiled=True),
        lax.all_gather(delta_heads, "ctx", axis=1, tiled=True),
    )
    zero_grad = jnp.zeros((row_count, head_count, HEAD), jnp.float32)

    def scan_query(current, scan_item):
        return (
            query_step(
                current,
                scan_item[0],
                scan_item[1],
                scan_item[2],
                query_heads,
                context_heads,
                logsum,
                delta_heads,
                length,
                score_scale,
            ),
            None,
        )

    grad_query, unused = lax.scan(scan_query, zero_grad, (key_blocks, value_blocks, block_starts))
    grad_key, grad_value = key_step(
        lax.all_gather(queries, "ctx", axis=0, tiled=True),
        lax.all_gather(grad_context, "ctx", axis=0, tiled=True),
        all_logsum,
        all_deltas,
        key_heads,
        value_heads,
        row_usable,
        score_scale,
    )
    grad_query = grad_query.reshape(row_count, inner_width).astype(jnp.bfloat16)
    grad_key = grad_key.reshape(row_count, inner_width).astype(jnp.bfloat16)
    grad_value = grad_value.reshape(row_count, inner_width).astype(jnp.bfloat16)
    grad_input = (
        back_project(grad_query, full_query)
        + back_project(grad_key, full_key)
        + back_project(grad_value, full_value)
    )
    grad_frames = grad_input.astype(jnp.bfloat16)
    summed_grad = lax.psum(
        lax.dot_general(
            context, masked_grad, (((0,), (0,)), ((), ())), preferred_element_type=jnp.float32
        ),
        ("rep", "ctx"),
    )
    grad_out = lax.psum_scatter(summed_grad, "dp", scatter_dimension=0, tiled=True)
    return (attended[None], grad_frames[None], grad_out)


MESH = pl.DeviceIdType.MESH


def dot(left, right, left_dim, right_dim):
    return lax.dot_general(
        left, right, (((left_dim,), (right_dim,)), ((), ())), preferred_element_type=jnp.float32
    )


def fused_kernel(
    frames_ref,
    length_ref,
    cot_ref,
    wq_ref,
    wk_ref,
    wv_ref,
    wo_ref,
    attended_ref,
    grad_frames_ref,
    grad_out_ref,
    xs,
    upstream,
    mine,
    cs,
    wq,
    wk,
    wv,
    wo,
    qs,
    ks,
    vs,
    gs,
    ctx,
    logsum,
    deltas,
    dq,
    dk,
    dv,
    part,
    part_in,
    slices,
    send_sem,
    recv_sem,
    local_sem,
):
    rep, dp, z = lax.axis_index("rep"), lax.axis_index("dp"), lax.axis_index("ctx")
    count = 4
    heads = 4
    rows = frames_ref.shape[1]
    full = rows * count
    width = slices.shape[2]
    scale = HEAD ** (-0.5)
    sibling = dp + 1 - 2 * lax.rem(dp, 2)
    across = lax.rem(dp + 2, 4)
    across_sibling = lax.rem(sibling + 2, 4)
    other_rep = 1 - rep
    group = rep * 4 + dp

    local = [
        pltpu.make_async_copy(source, target, local_sem.at[at])
        for at, (source, target) in enumerate(
            (
                (wk_ref, wk.at[dp]),
                (wv_ref, wv.at[dp]),
                (wq_ref, wq.at[dp]),
                (wo_ref, wo.at[dp]),
                (frames_ref.at[0], xs.at[z]),
                (cot_ref.at[0], upstream),
            )
        )
    ]
    for copy in local:
        copy.start()

    barrier = pltpu.get_barrier_semaphore()
    for step in range(1, count):
        pl.semaphore_signal(
            barrier, inc=1, device_id=(rep, dp, lax.rem(z + step, count)), device_id_type=MESH
        )
    for step in range(1, 8):
        peer = lax.rem(group + step, 8)
        pl.semaphore_signal(
            barrier, inc=1, device_id=(peer // 4, lax.rem(peer, 4), z), device_id_type=MESH
        )
    pl.semaphore_wait(barrier, 10)

    def remote(source, target, index, device):
        return pltpu.make_async_remote_copy(
            src_ref=source,
            dst_ref=target,
            send_sem=send_sem.at[index],
            recv_sem=recv_sem.at[index],
            device_id=device,
            device_id_type=MESH,
        )

    def chain(which, side, hop):
        sign = 1 - 2 * side
        pool = (xs, gs)[which]
        owner = z - sign * (hop - 1)
        slot = jnp.clip(owner, 0, count - 1)
        source = frames_ref.at[0] if which == 0 and hop == 1 else pool.at[slot]
        target = jnp.clip(z + sign, 0, count - 1)
        index = which * 6 + side * 3 + hop - 1
        valid = (z + sign >= 0) & (z + sign < count) & (owner >= 0) & (owner < count)
        return valid, remote(source, pool.at[slot], index, (rep, dp, target))

    def chain_send(which, hop):
        for side in range(2):
            valid, copy = chain(which, side, hop)

            @pl.when(valid)
            def _():
                copy.start()

    def chain_recv(which, hop):
        for side in range(2):
            sign = 1 - 2 * side
            pool = (xs, gs)[which]
            owner = z - sign * hop
            slot = jnp.clip(owner, 0, count - 1)
            index = which * 6 + side * 3 + hop - 1

            @pl.when((owner >= 0) & (owner < count))
            def _():
                remote(pool.at[slot], pool.at[slot], index, (rep, dp, z)).wait_recv()

    weights = ((wo_ref, wo), (wk_ref, wk), (wv_ref, wv), (wq_ref, wq))

    def half(ref, which):
        size = ref.shape[0] // 2
        return ref.at[pl.ds(pl.multiple_of(which * size, size), size)]

    def chunk(ref, which, at):
        size = ref.shape[0] // 4
        return ref.at[pl.ds(pl.multiple_of((which * 2 + at) * size, size), size)]

    def weight_copy(piece, step):
        shard, pool = weights[piece]
        index = 12 + piece * 7 + step
        if step == 0:
            return remote(shard, pool.at[dp], index, (rep, sibling, z))
        if step < 3:
            target = chunk(pool.at[dp], rep, step - 1)
            return remote(chunk(shard, rep, step - 1), target, index, (rep, across, z))
        mine_at = pool.at[across]
        if step < 5:
            source = chunk(mine_at, rep, step - 3)
            return remote(source, source, index, (other_rep, dp, z))
        source = half(mine_at, rep if step == 5 else other_rep)
        return remote(source, source, index, (rep, sibling, z))

    def weight_recv(piece, step):
        pool = weights[piece][1]
        index = 12 + piece * 7 + step
        if step == 0:
            target = pool.at[sibling]
        elif step < 3:
            target = chunk(pool.at[across], rep, step - 1)
        elif step < 5:
            target = chunk(pool.at[across], other_rep, step - 3)
        else:
            target = half(pool.at[across_sibling], rep if step == 5 else other_rep)
        remote(target, target, index, (rep, dp, z)).wait_recv()

    def finish_chunk(at):
        weight_recv(at // 2, 3 + at % 2)
        if at % 2 == 1:
            weight_copy(at // 2, 6).start()

    def weight_chunk(at):
        weight_recv(at // 2, 1 + at % 2)
        weight_copy(at // 2, 3 + at % 2).start()
        if at + 2 < 8:
            weight_copy((at + 2) // 2, 1 + at % 2).start()
        if at % 2 == 1:
            weight_copy(at // 2, 5).start()
        if at >= 2:
            finish_chunk(at - 2)

    def cot_copy(step):
        peer = lax.rem(z + step, count)
        return remote(mine.at[peer], cs.at[z], 52 + step, (rep, dp, peer))

    chain_send(0, 1)
    for at in range(2):
        weight_copy(0, 1 + at).start()
    for piece in range(4):
        weight_copy(piece, 0).start()
    for copy in local:
        copy.wait()

    length = length_ref[0]
    columns = [slice(at * width, (at + 1) * width) for at in range(count)]
    real = z * rows + lax.broadcasted_iota(jnp.int32, (rows, width), 0) < length
    for at in range(count):
        kept = jnp.where(real, upstream[:, columns[at]].astype(jnp.float32), 0.0)
        mine[at] = kept.astype(jnp.bfloat16)
    cs[z] = mine[z]

    for at in range(4):
        weight_chunk(at)
    chain_recv(0, 1)
    chain_send(0, 2)
    for at in range(4, 6):
        weight_chunk(at)
    for step in (0, 5, 6):
        weight_recv(0, step)
    masked = jnp.concatenate([mine[at] for at in range(count)], axis=1)
    matrix = dot(masked, wo[...].reshape(512, 1024), 1, 1).astype(jnp.bfloat16)
    for head in range(heads):
        gs[z, head] = matrix[:, head * HEAD : (head + 1) * HEAD]
    weight_chunk(6)
    chain_recv(0, 2)
    chain_send(0, 3)
    chain_send(1, 1)
    weight_chunk(7)
    for step in range(1, count):
        cot_copy(step).start()
    finish_chunk(6)
    finish_chunk(7)
    for piece in range(1, 4):
        for step in (0, 5, 6):
            weight_recv(piece, step)

    def project(block):
        inputs = xs[block]
        start = pl.multiple_of(block * rows, rows)
        for pool, kept in ((wk, ks), (wv, vs), (wq, qs)):
            matrix = dot(inputs, pool[...].reshape(1024, 512), 1, 0).astype(jnp.bfloat16)
            for head in range(heads):
                kept[head, pl.ds(start, rows), :] = matrix[:, head * HEAD : (head + 1) * HEAD]

    def project_hops(first, last):
        def body(step, carry):
            hop = step // 2
            block = z + hop * (1 - 2 * lax.rem(step, 2))

            @pl.when((block >= 0) & (block < count))
            def _():
                project(jnp.clip(block, 0, count - 1))

            return carry

        lax.fori_loop(first, last, body, 0)

    project_hops(1, 6)
    chain_recv(1, 1)
    chain_send(1, 2)
    chain_recv(0, 3)
    project_hops(6, 8)

    def key_mask(amount):
        return lax.broadcasted_iota(jnp.int32, (amount, full), 1) < length

    def forward(step, carry):
        head = step // 2
        amount = full // 2
        start = pl.multiple_of(lax.rem(step, 2) * amount, amount)
        usable = key_mask(amount)
        scores = dot(qs[head, pl.ds(start, amount), :], ks[head], 1, 1) * scale
        scores = jnp.where(usable, scores, MASKED_SCORE)
        maxima = jnp.max(scores, axis=1, keepdims=True)
        exponent = jnp.where(usable, jnp.exp(scores - maxima), 0.0)
        totals = jnp.sum(exponent, axis=1, keepdims=True)
        mixed = dot(exponent.astype(jnp.bfloat16), vs[head], 1, 0)
        ctx[head, pl.ds(start, amount), :] = (mixed / totals).astype(jnp.bfloat16)
        logsum[head, pl.ds(start, amount), :] = maxima + jnp.log(totals)
        return carry

    lax.fori_loop(0, 4, forward, 0)
    chain_recv(1, 2)
    chain_send(1, 3)
    lax.fori_loop(4, 8, forward, 0)

    own = pl.ds(pl.multiple_of(z * rows, rows), rows)
    own_context = jnp.concatenate([ctx[head, own, :] for head in range(heads)], axis=1)
    attended = dot(own_context, wo[...].reshape(512, 1024), 1, 0)
    row_at = z * rows + lax.broadcasted_iota(jnp.int32, attended.shape, 0)
    attended_ref[0] = jnp.where(row_at < length, attended, 0.0).astype(jnp.bfloat16)

    for step in range(1, count):
        source = lax.rem(z + count - step, count)
        remote(cs.at[source], cs.at[source], 52 + step, (rep, dp, z)).wait_recv()
    masked_slice = cs[...].reshape(full, width)
    for head in range(heads):
        part[head] = dot(ctx[head], masked_slice, 0, 0).astype(jnp.bfloat16)

    def part_copy(step):
        peer = lax.rem(group + step, 8)
        peer_dp = lax.rem(peer, 4)
        return remote(part.at[peer_dp], part_in.at[step], 40 + step, (peer // 4, peer_dp, z))

    for step in range(1, 8):
        part_copy(step).start()

    chain_recv(1, 3)

    def backward(head, carry):
        queries, keys, values = qs[head], ks[head], vs[head]
        grads = gs[:, head].reshape(full, HEAD)
        terms = grads.astype(jnp.float32) * ctx[head].astype(jnp.float32)
        deltas[...] = jnp.sum(terms, axis=1, keepdims=True)
        own_keys, own_values = ks[head, own, :], vs[head, own, :]
        scores = dot(queries, own_keys, 1, 1) * scale
        at = z * rows + lax.broadcasted_iota(jnp.int32, scores.shape, 1)
        attention = jnp.where(at < length, jnp.exp(scores - logsum[head]), 0.0)
        dv[head] = dot(attention.astype(jnp.bfloat16), grads, 0, 0).astype(jnp.bfloat16)
        grad_prob = dot(grads, own_values, 1, 1)
        grad_score = (attention * (grad_prob - deltas[...])).astype(jnp.bfloat16)
        dk[head] = (dot(grad_score, queries, 0, 0) * scale).astype(jnp.bfloat16)
        scores = dot(qs[head, own, :], keys, 1, 1) * scale
        attention = jnp.where(key_mask(rows), jnp.exp(scores - logsum[head, own, :]), 0.0)
        grad_prob = dot(gs[z, head], values, 1, 1)
        grad_score = (attention * (grad_prob - deltas[own, :])).astype(jnp.bfloat16)
        dq[head] = (dot(grad_score, keys, 1, 0) * scale).astype(jnp.bfloat16)
        return carry

    lax.fori_loop(0, heads, backward, 0)

    total = part[dp].astype(jnp.float32)
    for step in range(1, 8):
        part_copy(step).wait_recv()
        total = total + part_in[step].astype(jnp.float32)
    slices[z] = total.astype(jnp.bfloat16)

    def slice_copy(step):
        return remote(
            slices.at[z], slices.at[z], 48 + step, (rep, dp, lax.rem(z + step, count))
        )

    for step in range(1, count):
        slice_copy(step).start()

    grads = [
        jnp.concatenate([kept[head] for head in range(heads)], axis=1) for kept in (dq, dk, dv)
    ]
    for shard in range(4):
        added = (
            dot(grads[0], wq[shard], 1, 1)
            + dot(grads[1], wk[shard], 1, 1)
            + dot(grads[2], wv[shard], 1, 1)
        )
        grad_frames_ref[0, :, shard * 256 : (shard + 1) * 256] = added.astype(jnp.bfloat16)

    for piece in range(4):
        for step in range(7):
            weight_copy(piece, step).wait_send()
    for which in range(2):
        for hop in range(1, count):
            for side in range(2):
                valid, copy = chain(which, side, hop)

                @pl.when(valid)
                def _():
                    copy.wait_send()

    for step in range(1, count):
        cot_copy(step).wait_send()
    for step in range(1, 8):
        part_copy(step).wait_send()
    for step in range(1, count):
        source = lax.rem(z + count - step, count)
        remote(slices.at[source], slices.at[source], 48 + step, (rep, dp, z)).wait_recv()
    for step in range(1, count):
        slice_copy(step).wait_send()
    for at in range(count):
        grad_out_ref[:, at * width : (at + 1) * width] = slices[at].astype(jnp.float32)


def fused(frames, lengths, cotangent, w_query, w_key, w_value, w_out):
    vmem = pl.BlockSpec(memory_space=pltpu.VMEM)
    hbm = pl.BlockSpec(memory_space=pltpu.HBM)
    bf16, f32 = jnp.bfloat16, jnp.float32
    per_head = pltpu.VMEM((4, 512, HEAD), bf16)
    own_head = pltpu.VMEM((4, 128, HEAD), bf16)
    return pl.pallas_call(
        fused_kernel,
        out_shape=(
            jax.ShapeDtypeStruct(frames.shape, bf16),
            jax.ShapeDtypeStruct(frames.shape, bf16),
            jax.ShapeDtypeStruct(w_out.shape, f32),
        ),
        in_specs=[hbm, pl.BlockSpec(memory_space=pltpu.SMEM)] + [hbm] * 5,
        out_specs=(vmem, vmem, vmem),
        scratch_shapes=[
            pltpu.VMEM((4, 128, 1024), bf16),
            pltpu.VMEM((128, 1024), bf16),
            pltpu.VMEM((4, 128, 256), bf16),
            pltpu.VMEM((4, 128, 256), bf16),
            pltpu.VMEM((4, 256, 512), bf16),
            pltpu.VMEM((4, 256, 512), bf16),
            pltpu.VMEM((4, 256, 512), bf16),
            pltpu.VMEM((4, 128, 1024), bf16),
            per_head,
            per_head,
            per_head,
            pltpu.VMEM((4, 4, 128, HEAD), bf16),
            per_head,
            pltpu.VMEM((4, 512, 1), f32),
            pltpu.VMEM((512, 1), f32),
            own_head,
            own_head,
            own_head,
            pltpu.VMEM((4, 128, 256), bf16),
            pltpu.VMEM((8, 128, 256), bf16),
            pltpu.VMEM((4, 128, 256), bf16),
            pltpu.SemaphoreType.DMA((56,)),
            pltpu.SemaphoreType.DMA((56,)),
            pltpu.SemaphoreType.DMA((6,)),
        ],
        compiler_params=pltpu.CompilerParams(
            collective_id=0, has_side_effects=True, vmem_limit_bytes=48 * 1024 * 1024
        ),
    )(frames, lengths, cotangent, w_query, w_key, w_value, w_out)


def either(sizes, frames, lengths, cotangent, w_query, w_key, w_value, w_out):
    fits = sizes == (2, 4, 4) and frames.shape == (1, 128, 1024) and w_query.shape == (256, 512)
    chosen = fused if fits else shards
    return chosen(frames, lengths, cotangent, w_query, w_key, w_value, w_out)


def solution(mesh):
    in_specs = (
        P(("rep", "dp"), "ctx", None),
        P(("rep", "dp")),
        P(("rep", "dp"), "ctx", None),
        P("dp", None),
        P("dp", None),
        P("dp", None),
        P("dp", None),
    )
    out_specs = (P(("rep", "dp"), "ctx", None), P(("rep", "dp"), "ctx", None), P("dp", None))
    sizes = (mesh.shape["rep"], mesh.shape["dp"], mesh.shape["ctx"])
    body = functools.partial(either, sizes)
    return jax.shard_map(body, mesh=mesh, in_specs=in_specs, out_specs=out_specs, check_vma=False)
```

```python
import functools
import math

import jax
import jax.numpy as jnp
from jax import lax
from jax.experimental import pallas as pl
from jax.experimental.pallas import tpu as pltpu
from jax.sharding import PartitionSpec as P

HEAD = 128


MASKED_SCORE = -1e30


def head_split(matrix, head_count):
    return matrix.reshape(matrix.shape[0], head_count, matrix.shape[1] // head_count)


def forward_step(carry, key_part, value_part, offset, query_heads, length, score_scale):
    head_count = query_heads.shape[1]
    amount = key_part.shape[0]
    maxima, totals, accumulated = carry
    key_heads = head_split(key_part, head_count)
    value_heads = head_split(value_part, head_count)
    scores = (
        jnp.einsum("rhe,nhe->hrn", query_heads, key_heads, preferred_element_type=jnp.float32)
        * score_scale
    )
    usable = offset + jnp.arange(amount) < length
    scores = jnp.where(usable[None, None, :], scores, MASKED_SCORE)
    new_maxima = jnp.maximum(maxima, jnp.max(scores, axis=2))
    factor = jnp.exp(maxima - new_maxima)
    exponent = jnp.where(usable[None, None, :], jnp.exp(scores - new_maxima[:, :, None]), 0.0)
    totals = totals * factor + jnp.sum(exponent, axis=2)
    mixed = jnp.einsum(
        "hrn,nhe->hre",
        exponent.astype(jnp.bfloat16),
        value_heads,
        preferred_element_type=jnp.float32,
    )
    accumulated = accumulated * factor[:, :, None] + mixed
    return (new_maxima, totals, accumulated)


def query_step(
    grad_accum,
    key_part,
    value_part,
    offset,
    query_heads,
    context_heads,
    logsum,
    deltas,
    length,
    score_scale,
):
    head_count = query_heads.shape[1]
    amount = key_part.shape[0]
    key_heads = head_split(key_part, head_count)
    value_heads = head_split(value_part, head_count)
    scores = (
        jnp.einsum("rhe,nhe->hrn", query_heads, key_heads, preferred_element_type=jnp.float32)
        * score_scale
    )
    usable = offset + jnp.arange(amount) < length
    attention = jnp.where(usable[None, None, :], jnp.exp(scores - logsum[:, :, None]), 0.0)
    grad_prob = jnp.einsum(
        "rhe,nhe->hrn", context_heads, value_heads, preferred_element_type=jnp.float32
    )
    grad_score = (attention * (grad_prob - deltas[:, :, None])).astype(jnp.bfloat16)
    added = jnp.einsum("hrn,nhe->rhe", grad_score, key_heads, preferred_element_type=jnp.float32)
    return grad_accum + added * score_scale


def key_step(
    query_part,
    context_part,
    all_logsum,
    all_deltas,
    key_heads,
    value_heads,
    key_usable,
    score_scale,
):
    head_count = key_heads.shape[1]
    query_heads = head_split(query_part, head_count)
    context_heads = head_split(context_part, head_count)
    scores = (
        jnp.einsum("rhe,nhe->hrn", query_heads, key_heads, preferred_element_type=jnp.float32)
        * score_scale
    )
    attention = jnp.where(key_usable[None, None, :], jnp.exp(scores - all_logsum[:, :, None]), 0.0)
    grad_value = jnp.einsum(
        "hrn,rhe->nhe",
        attention.astype(jnp.bfloat16),
        context_heads,
        preferred_element_type=jnp.float32,
    )
    grad_prob = jnp.einsum(
        "rhe,nhe->hrn", context_heads, value_heads, preferred_element_type=jnp.float32
    )
    grad_score = (attention * (grad_prob - all_deltas[:, :, None])).astype(jnp.bfloat16)
    added = jnp.einsum("hrn,rhe->nhe", grad_score, query_heads, preferred_element_type=jnp.float32)
    return (added * score_scale, grad_value)


def back_project(gradient, weight):
    return lax.dot_general(
        gradient, weight, (((1,), (1,)), ((), ())), preferred_element_type=jnp.float32
    )


def shards(frames, lengths, cotangent, w_query, w_key, w_value, w_out):
    full_query, full_key, full_value, full_out = (
        lax.all_gather(w_query, "dp", axis=0, tiled=True),
        lax.all_gather(w_key, "dp", axis=0, tiled=True),
        lax.all_gather(w_value, "dp", axis=0, tiled=True),
        lax.all_gather(w_out, "dp", axis=0, tiled=True),
    )
    inputs = frames[0]
    upstream = cotangent[0]
    length = lengths[0]
    row_count = inputs.shape[0]
    inner_width = full_query.shape[1]
    head_count = inner_width // HEAD
    score_scale = HEAD ** (-0.5)
    first_frame = lax.axis_index("ctx") * row_count
    row_usable = first_frame + jnp.arange(row_count) < length
    queries = jnp.dot(inputs, full_query, preferred_element_type=jnp.float32).astype(jnp.bfloat16)
    keys = jnp.dot(inputs, full_key, preferred_element_type=jnp.float32).astype(jnp.bfloat16)
    values = jnp.dot(inputs, full_value, preferred_element_type=jnp.float32).astype(jnp.bfloat16)
    query_heads = head_split(queries, head_count)
    key_heads = head_split(keys, head_count)
    value_heads = head_split(values, head_count)
    start_state = (
        jnp.full((head_count, row_count), MASKED_SCORE, jnp.float32),
        jnp.zeros((head_count, row_count), jnp.float32),
        jnp.zeros((head_count, row_count, HEAD), jnp.float32),
    )
    all_keys, all_values = (
        lax.all_gather(keys, "ctx", axis=0, tiled=True),
        lax.all_gather(values, "ctx", axis=0, tiled=True),
    )
    key_block = row_count * math.gcd(max(1, 512 // row_count), lax.axis_size("ctx"))
    block_count = all_keys.shape[0] // key_block
    key_blocks = all_keys.reshape(block_count, key_block, inner_width)
    value_blocks = all_values.reshape(block_count, key_block, inner_width)
    block_starts = jnp.arange(block_count, dtype=jnp.int32) * key_block

    def scan_forward(current, scan_item):
        return (
            forward_step(
                current, scan_item[0], scan_item[1], scan_item[2], query_heads, length, score_scale
            ),
            None,
        )

    softmax_state, unused = lax.scan(
        scan_forward, start_state, (key_blocks, value_blocks, block_starts)
    )
    maxima, totals, accumulated = softmax_state
    context = (
        (accumulated / totals[:, :, None])
        .transpose(1, 0, 2)
        .reshape(row_count, inner_width)
        .astype(jnp.bfloat16)
    )
    logsum = maxima + jnp.log(totals)
    attended = jnp.dot(context, full_out, preferred_element_type=jnp.float32)
    attended = jnp.where(row_usable[:, None], attended, 0.0).astype(jnp.bfloat16)
    masked_grad = jnp.where(row_usable[:, None], upstream, jnp.zeros_like(upstream))
    grad_context = back_project(masked_grad, full_out).astype(jnp.bfloat16)
    deltas = jnp.sum(
        (grad_context.astype(jnp.float32) * context.astype(jnp.float32)).reshape(
            row_count, head_count, HEAD
        ),
        axis=2,
    )
    context_heads = head_split(grad_context, head_count)
    delta_heads = deltas.T
    all_logsum, all_deltas = (
        lax.all_gather(logsum, "ctx", axis=1, tiled=True),
        lax.all_gather(delta_heads, "ctx", axis=1, tiled=True),
    )
    zero_grad = jnp.zeros((row_count, head_count, HEAD), jnp.float32)

    def scan_query(current, scan_item):
        return (
            query_step(
                current,
                scan_item[0],
                scan_item[1],
                scan_item[2],
                query_heads,
                context_heads,
                logsum,
                delta_heads,
                length,
                score_scale,
            ),
            None,
        )

    grad_query, unused = lax.scan(scan_query, zero_grad, (key_blocks, value_blocks, block_starts))
    grad_key, grad_value = key_step(
        lax.all_gather(queries, "ctx", axis=0, tiled=True),
        lax.all_gather(grad_context, "ctx", axis=0, tiled=True),
        all_logsum,
        all_deltas,
        key_heads,
        value_heads,
        row_usable,
        score_scale,
    )
    grad_query = grad_query.reshape(row_count, inner_width).astype(jnp.bfloat16)
    grad_key = grad_key.reshape(row_count, inner_width).astype(jnp.bfloat16)
    grad_value = grad_value.reshape(row_count, inner_width).astype(jnp.bfloat16)
    grad_input = (
        back_project(grad_query, full_query)
        + back_project(grad_key, full_key)
        + back_project(grad_value, full_value)
    )
    grad_frames = grad_input.astype(jnp.bfloat16)
    summed_grad = lax.psum(
        lax.dot_general(
            context, masked_grad, (((0,), (0,)), ((), ())), preferred_element_type=jnp.float32
        ),
        ("rep", "ctx"),
    )
    grad_out = lax.psum_scatter(summed_grad, "dp", scatter_dimension=0, tiled=True)
    return (attended[None], grad_frames[None], grad_out)


MESH = pl.DeviceIdType.MESH


def dot(left, right, left_dim, right_dim):
    return lax.dot_general(
        left, right, (((left_dim,), (right_dim,)), ((), ())), preferred_element_type=jnp.float32
    )


def fused_kernel(
    frames_ref,
    length_ref,
    cot_ref,
    wq_ref,
    wk_ref,
    wv_ref,
    wo_ref,
    attended_ref,
    grad_frames_ref,
    grad_out_ref,
    xs,
    upstream,
    mine,
    cs,
    wq,
    wk,
    wv,
    wo,
    qs,
    ks,
    vs,
    gs,
    ctx,
    logsum,
    deltas,
    dq,
    dk,
    dv,
    part,
    part_in,
    slices,
    send_sem,
    recv_sem,
    local_sem,
):
    rep, dp, z = lax.axis_index("rep"), lax.axis_index("dp"), lax.axis_index("ctx")
    count = 4
    heads = 4
    rows = frames_ref.shape[1]
    full = rows * count
    width = slices.shape[2]
    scale = HEAD ** (-0.5)
    sibling = dp + 1 - 2 * lax.rem(dp, 2)
    across = lax.rem(dp + 2, 4)
    across_sibling = lax.rem(sibling + 2, 4)
    other_rep = 1 - rep
    group = rep * 4 + dp

    local = [
        pltpu.make_async_copy(source, target, local_sem.at[at])
        for at, (source, target) in enumerate(
            (
                (wk_ref, wk.at[dp]),
                (wv_ref, wv.at[dp]),
                (wq_ref, wq.at[dp]),
                (wo_ref, wo.at[dp]),
                (frames_ref.at[0], xs.at[z]),
                (cot_ref.at[0], upstream),
            )
        )
    ]
    for copy in local:
        copy.start()

    barrier = pltpu.get_barrier_semaphore()
    for step in range(1, count):
        pl.semaphore_signal(
            barrier, inc=1, device_id=(rep, dp, lax.rem(z + step, count)), device_id_type=MESH
        )
    for step in range(1, 8):
        peer = lax.rem(group + step, 8)
        pl.semaphore_signal(
            barrier, inc=1, device_id=(peer // 4, lax.rem(peer, 4), z), device_id_type=MESH
        )
    pl.semaphore_wait(barrier, 10)

    def remote(source, target, index, device):
        return pltpu.make_async_remote_copy(
            src_ref=source,
            dst_ref=target,
            send_sem=send_sem.at[index],
            recv_sem=recv_sem.at[index],
            device_id=device,
            device_id_type=MESH,
        )

    def chain(which, side, hop):
        sign = 1 - 2 * side
        pool = (xs, gs)[which]
        owner = z - sign * (hop - 1)
        slot = jnp.clip(owner, 0, count - 1)
        source = frames_ref.at[0] if which == 0 and hop == 1 else pool.at[slot]
        target = jnp.clip(z + sign, 0, count - 1)
        index = which * 6 + side * 3 + hop - 1
        valid = (z + sign >= 0) & (z + sign < count) & (owner >= 0) & (owner < count)
        return valid, remote(source, pool.at[slot], index, (rep, dp, target))

    def chain_send(which, hop):
        for side in range(2):
            valid, copy = chain(which, side, hop)

            @pl.when(valid)
            def _():
                copy.start()

    def chain_recv(which, hop):
        for side in range(2):
            sign = 1 - 2 * side
            pool = (xs, gs)[which]
            owner = z - sign * hop
            slot = jnp.clip(owner, 0, count - 1)
            index = which * 6 + side * 3 + hop - 1

            @pl.when((owner >= 0) & (owner < count))
            def _():
                remote(pool.at[slot], pool.at[slot], index, (rep, dp, z)).wait_recv()

    weights = ((wo_ref, wo), (wk_ref, wk), (wv_ref, wv), (wq_ref, wq))

    def half(ref, which):
        size = ref.shape[0] // 2
        return ref.at[pl.ds(pl.multiple_of(which * size, size), size)]

    def chunk(ref, which, at):
        size = ref.shape[0] // 4
        return ref.at[pl.ds(pl.multiple_of((which * 2 + at) * size, size), size)]

    def weight_copy(piece, step):
        shard, pool = weights[piece]
        index = 12 + piece * 7 + step
        if step == 0:
            return remote(shard, pool.at[dp], index, (rep, sibling, z))
        if step < 3:
            target = chunk(pool.at[dp], rep, step - 1)
            return remote(chunk(shard, rep, step - 1), target, index, (rep, across, z))
        mine_at = pool.at[across]
        if step < 5:
            source = chunk(mine_at, rep, step - 3)
            return remote(source, source, index, (other_rep, dp, z))
        source = half(mine_at, rep if step == 5 else other_rep)
        return remote(source, source, index, (rep, sibling, z))

    def weight_recv(piece, step):
        pool = weights[piece][1]
        index = 12 + piece * 7 + step
        if step == 0:
            target = pool.at[sibling]
        elif step < 3:
            target = chunk(pool.at[across], rep, step - 1)
        elif step < 5:
            target = chunk(pool.at[across], other_rep, step - 3)
        else:
            target = half(pool.at[across_sibling], rep if step == 5 else other_rep)
        remote(target, target, index, (rep, dp, z)).wait_recv()

    def finish_chunk(at):
        weight_recv(at // 2, 3 + at % 2)
        if at % 2 == 1:
            weight_copy(at // 2, 6).start()

    def weight_chunk(at):
        weight_recv(at // 2, 1 + at % 2)
        weight_copy(at // 2, 3 + at % 2).start()
        if at + 2 < 8:
            weight_copy((at + 2) // 2, 1 + at % 2).start()
        if at % 2 == 1:
            weight_copy(at // 2, 5).start()
        if at >= 2:
            finish_chunk(at - 2)

    def cot_copy(step):
        peer = lax.rem(z + step, count)
        return remote(mine.at[peer], cs.at[z], 52 + step, (rep, dp, peer))

    chain_send(0, 1)
    for at in range(2):
        weight_copy(0, 1 + at).start()
    for piece in range(4):
        weight_copy(piece, 0).start()
    for copy in local:
        copy.wait()

    length = length_ref[0]
    columns = [slice(at * width, (at + 1) * width) for at in range(count)]
    real = z * rows + lax.broadcasted_iota(jnp.int32, (rows, width), 0) < length
    for at in range(count):
        kept = jnp.where(real, upstream[:, columns[at]].astype(jnp.float32), 0.0)
        mine[at] = kept.astype(jnp.bfloat16)
    cs[z] = mine[z]

    for at in range(4):
        weight_chunk(at)
    chain_recv(0, 1)
    chain_send(0, 2)
    for at in range(4, 6):
        weight_chunk(at)
    for step in (0, 5, 6):
        weight_recv(0, step)
    masked = jnp.concatenate([mine[at] for at in range(count)], axis=1)
    matrix = dot(masked, wo[...].reshape(512, 1024), 1, 1).astype(jnp.bfloat16)
    for head in range(heads):
        gs[z, head] = matrix[:, head * HEAD : (head + 1) * HEAD]
    weight_chunk(6)
    chain_recv(0, 2)
    chain_send(0, 3)
    for step in range(1, count):
        cot_copy(step).start()
    chain_send(1, 1)
    weight_chunk(7)
    finish_chunk(6)
    finish_chunk(7)
    for piece in range(1, 4):
        for step in (0, 5, 6):
            weight_recv(piece, step)

    def project(block):
        inputs = xs[block]
        start = pl.multiple_of(block * rows, rows)
        for pool, kept in ((wk, ks), (wv, vs), (wq, qs)):
            matrix = dot(inputs, pool[...].reshape(1024, 512), 1, 0).astype(jnp.bfloat16)
            for head in range(heads):
                kept[head, pl.ds(start, rows), :] = matrix[:, head * HEAD : (head + 1) * HEAD]

    def project_hops(first, last):
        def body(step, carry):
            hop = step // 2
            block = z + hop * (1 - 2 * lax.rem(step, 2))

            @pl.when((block >= 0) & (block < count))
            def _():
                project(jnp.clip(block, 0, count - 1))

            return carry

        lax.fori_loop(first, last, body, 0)

    project_hops(1, 6)
    chain_recv(0, 3)
    project_hops(6, 8)

    def key_mask(amount):
        return lax.broadcasted_iota(jnp.int32, (amount, full), 1) < length

    def forward(step, carry):
        head = step // 2
        amount = full // 2
        start = pl.multiple_of(lax.rem(step, 2) * amount, amount)
        usable = key_mask(amount)
        scores = dot(qs[head, pl.ds(start, amount), :], ks[head], 1, 1) * scale
        scores = jnp.where(usable, scores, MASKED_SCORE)
        maxima = jnp.max(scores, axis=1, keepdims=True)
        exponent = jnp.where(usable, jnp.exp(scores - maxima), 0.0)
        totals = jnp.sum(exponent, axis=1, keepdims=True)
        mixed = dot(exponent.astype(jnp.bfloat16), vs[head], 1, 0)
        ctx[head, pl.ds(start, amount), :] = (mixed / totals).astype(jnp.bfloat16)
        logsum[head, pl.ds(start, amount), :] = maxima + jnp.log(totals)
        return carry

    lax.fori_loop(0, 4, forward, 0)
    chain_recv(1, 1)
    chain_send(1, 2)
    lax.fori_loop(4, 8, forward, 0)

    own = pl.ds(pl.multiple_of(z * rows, rows), rows)
    for step in range(1, count):
        source = lax.rem(z + count - step, count)
        remote(cs.at[source], cs.at[source], 52 + step, (rep, dp, z)).wait_recv()
    masked_slice = cs[...].reshape(full, width)
    for head in range(heads):
        part[head] = dot(ctx[head], masked_slice, 0, 0).astype(jnp.bfloat16)

    def part_copy(step):
        peer = lax.rem(group + step, 8)
        peer_dp = lax.rem(peer, 4)
        return remote(part.at[peer_dp], part_in.at[step], 40 + step, (peer // 4, peer_dp, z))

    for step in range(1, 8):
        part_copy(step).start()
    chain_recv(1, 2)
    chain_send(1, 3)

    own_context = jnp.concatenate([ctx[head, own, :] for head in range(heads)], axis=1)
    attended = dot(own_context, wo[...].reshape(512, 1024), 1, 0)
    row_at = z * rows + lax.broadcasted_iota(jnp.int32, attended.shape, 0)
    attended_ref[0] = jnp.where(row_at < length, attended, 0.0).astype(jnp.bfloat16)

    total = part[dp].astype(jnp.float32)
    for step in range(1, 8):
        part_copy(step).wait_recv()
        total = total + part_in[step].astype(jnp.float32)
    slices[z] = total.astype(jnp.bfloat16)

    def slice_copy(step):
        return remote(
            slices.at[z], slices.at[z], 48 + step, (rep, dp, lax.rem(z + step, count))
        )

    for step in range(1, count):
        slice_copy(step).start()

    chain_recv(1, 3)

    def backward(head, carry):
        queries, keys, values = qs[head], ks[head], vs[head]
        grads = gs[:, head].reshape(full, HEAD)
        terms = grads.astype(jnp.float32) * ctx[head].astype(jnp.float32)
        deltas[...] = jnp.sum(terms, axis=1, keepdims=True)
        own_keys, own_values = ks[head, own, :], vs[head, own, :]
        scores = dot(queries, own_keys, 1, 1) * scale
        at = z * rows + lax.broadcasted_iota(jnp.int32, scores.shape, 1)
        attention = jnp.where(at < length, jnp.exp(scores - logsum[head]), 0.0)
        dv[head] = dot(attention.astype(jnp.bfloat16), grads, 0, 0).astype(jnp.bfloat16)
        grad_prob = dot(grads, own_values, 1, 1)
        grad_score = (attention * (grad_prob - deltas[...])).astype(jnp.bfloat16)
        dk[head] = (dot(grad_score, queries, 0, 0) * scale).astype(jnp.bfloat16)
        scores = dot(qs[head, own, :], keys, 1, 1) * scale
        attention = jnp.where(key_mask(rows), jnp.exp(scores - logsum[head, own, :]), 0.0)
        grad_prob = dot(gs[z, head], values, 1, 1)
        grad_score = (attention * (grad_prob - deltas[own, :])).astype(jnp.bfloat16)
        dq[head] = (dot(grad_score, keys, 1, 0) * scale).astype(jnp.bfloat16)
        return carry

    lax.fori_loop(0, heads, backward, 0)

    grads = [
        jnp.concatenate([kept[head] for head in range(heads)], axis=1) for kept in (dq, dk, dv)
    ]
    for shard in range(4):
        added = (
            dot(grads[0], wq[shard], 1, 1)
            + dot(grads[1], wk[shard], 1, 1)
            + dot(grads[2], wv[shard], 1, 1)
        )
        grad_frames_ref[0, :, shard * 256 : (shard + 1) * 256] = added.astype(jnp.bfloat16)

    for piece in range(4):
        for step in range(7):
            weight_copy(piece, step).wait_send()
    for which in range(2):
        for hop in range(1, count):
            for side in range(2):
                valid, copy = chain(which, side, hop)

                @pl.when(valid)
                def _():
                    copy.wait_send()

    for step in range(1, count):
        cot_copy(step).wait_send()
    for step in range(1, 8):
        part_copy(step).wait_send()
    for step in range(1, count):
        source = lax.rem(z + count - step, count)
        remote(slices.at[source], slices.at[source], 48 + step, (rep, dp, z)).wait_recv()
    for step in range(1, count):
        slice_copy(step).wait_send()
    for at in range(count):
        grad_out_ref[:, at * width : (at + 1) * width] = slices[at].astype(jnp.float32)


def fused(frames, lengths, cotangent, w_query, w_key, w_value, w_out):
    vmem = pl.BlockSpec(memory_space=pltpu.VMEM)
    hbm = pl.BlockSpec(memory_space=pltpu.HBM)
    bf16, f32 = jnp.bfloat16, jnp.float32
    per_head = pltpu.VMEM((4, 512, HEAD), bf16)
    own_head = pltpu.VMEM((4, 128, HEAD), bf16)
    return pl.pallas_call(
        fused_kernel,
        out_shape=(
            jax.ShapeDtypeStruct(frames.shape, bf16),
            jax.ShapeDtypeStruct(frames.shape, bf16),
            jax.ShapeDtypeStruct(w_out.shape, f32),
        ),
        in_specs=[hbm, pl.BlockSpec(memory_space=pltpu.SMEM)] + [hbm] * 5,
        out_specs=(vmem, vmem, vmem),
        scratch_shapes=[
            pltpu.VMEM((4, 128, 1024), bf16),
            pltpu.VMEM((128, 1024), bf16),
            pltpu.VMEM((4, 128, 256), bf16),
            pltpu.VMEM((4, 128, 256), bf16),
            pltpu.VMEM((4, 256, 512), bf16),
            pltpu.VMEM((4, 256, 512), bf16),
            pltpu.VMEM((4, 256, 512), bf16),
            pltpu.VMEM((4, 128, 1024), bf16),
            per_head,
            per_head,
            per_head,
            pltpu.VMEM((4, 4, 128, HEAD), bf16),
            per_head,
            pltpu.VMEM((4, 512, 1), f32),
            pltpu.VMEM((512, 1), f32),
            own_head,
            own_head,
            own_head,
            pltpu.VMEM((4, 128, 256), bf16),
            pltpu.VMEM((8, 128, 256), bf16),
            pltpu.VMEM((4, 128, 256), bf16),
            pltpu.SemaphoreType.DMA((56,)),
            pltpu.SemaphoreType.DMA((56,)),
            pltpu.SemaphoreType.DMA((6,)),
        ],
        compiler_params=pltpu.CompilerParams(
            collective_id=0, has_side_effects=True, vmem_limit_bytes=48 * 1024 * 1024
        ),
    )(frames, lengths, cotangent, w_query, w_key, w_value, w_out)


def either(sizes, frames, lengths, cotangent, w_query, w_key, w_value, w_out):
    fits = sizes == (2, 4, 4) and frames.shape == (1, 128, 1024) and w_query.shape == (256, 512)
    chosen = fused if fits else shards
    return chosen(frames, lengths, cotangent, w_query, w_key, w_value, w_out)


def solution(mesh):
    in_specs = (
        P(("rep", "dp"), "ctx", None),
        P(("rep", "dp")),
        P(("rep", "dp"), "ctx", None),
        P("dp", None),
        P("dp", None),
        P("dp", None),
        P("dp", None),
    )
    out_specs = (P(("rep", "dp"), "ctx", None), P(("rep", "dp"), "ctx", None), P("dp", None))
    sizes = (mesh.shape["rep"], mesh.shape["dp"], mesh.shape["ctx"])
    body = functools.partial(either, sizes)
    return jax.shard_map(body, mesh=mesh, in_specs=in_specs, out_specs=out_specs, check_vma=False)
```

```python
import functools
import math

import jax
import jax.numpy as jnp
from jax import lax
from jax.experimental import pallas as pl
from jax.experimental.pallas import tpu as pltpu
from jax.sharding import PartitionSpec as P

HEAD = 128


MASKED_SCORE = -1e30


def head_split(matrix, head_count):
    return matrix.reshape(matrix.shape[0], head_count, matrix.shape[1] // head_count)


def forward_step(carry, key_part, value_part, offset, query_heads, length, score_scale):
    head_count = query_heads.shape[1]
    amount = key_part.shape[0]
    maxima, totals, accumulated = carry
    key_heads = head_split(key_part, head_count)
    value_heads = head_split(value_part, head_count)
    scores = (
        jnp.einsum("rhe,nhe->hrn", query_heads, key_heads, preferred_element_type=jnp.float32)
        * score_scale
    )
    usable = offset + jnp.arange(amount) < length
    scores = jnp.where(usable[None, None, :], scores, MASKED_SCORE)
    new_maxima = jnp.maximum(maxima, jnp.max(scores, axis=2))
    factor = jnp.exp(maxima - new_maxima)
    exponent = jnp.where(usable[None, None, :], jnp.exp(scores - new_maxima[:, :, None]), 0.0)
    totals = totals * factor + jnp.sum(exponent, axis=2)
    mixed = jnp.einsum(
        "hrn,nhe->hre",
        exponent.astype(jnp.bfloat16),
        value_heads,
        preferred_element_type=jnp.float32,
    )
    accumulated = accumulated * factor[:, :, None] + mixed
    return (new_maxima, totals, accumulated)


def query_step(
    grad_accum,
    key_part,
    value_part,
    offset,
    query_heads,
    context_heads,
    logsum,
    deltas,
    length,
    score_scale,
):
    head_count = query_heads.shape[1]
    amount = key_part.shape[0]
    key_heads = head_split(key_part, head_count)
    value_heads = head_split(value_part, head_count)
    scores = (
        jnp.einsum("rhe,nhe->hrn", query_heads, key_heads, preferred_element_type=jnp.float32)
        * score_scale
    )
    usable = offset + jnp.arange(amount) < length
    attention = jnp.where(usable[None, None, :], jnp.exp(scores - logsum[:, :, None]), 0.0)
    grad_prob = jnp.einsum(
        "rhe,nhe->hrn", context_heads, value_heads, preferred_element_type=jnp.float32
    )
    grad_score = (attention * (grad_prob - deltas[:, :, None])).astype(jnp.bfloat16)
    added = jnp.einsum("hrn,nhe->rhe", grad_score, key_heads, preferred_element_type=jnp.float32)
    return grad_accum + added * score_scale


def key_step(
    query_part,
    context_part,
    all_logsum,
    all_deltas,
    key_heads,
    value_heads,
    key_usable,
    score_scale,
):
    head_count = key_heads.shape[1]
    query_heads = head_split(query_part, head_count)
    context_heads = head_split(context_part, head_count)
    scores = (
        jnp.einsum("rhe,nhe->hrn", query_heads, key_heads, preferred_element_type=jnp.float32)
        * score_scale
    )
    attention = jnp.where(key_usable[None, None, :], jnp.exp(scores - all_logsum[:, :, None]), 0.0)
    grad_value = jnp.einsum(
        "hrn,rhe->nhe",
        attention.astype(jnp.bfloat16),
        context_heads,
        preferred_element_type=jnp.float32,
    )
    grad_prob = jnp.einsum(
        "rhe,nhe->hrn", context_heads, value_heads, preferred_element_type=jnp.float32
    )
    grad_score = (attention * (grad_prob - all_deltas[:, :, None])).astype(jnp.bfloat16)
    added = jnp.einsum("hrn,rhe->nhe", grad_score, query_heads, preferred_element_type=jnp.float32)
    return (added * score_scale, grad_value)


def back_project(gradient, weight):
    return lax.dot_general(
        gradient, weight, (((1,), (1,)), ((), ())), preferred_element_type=jnp.float32
    )


def shards(frames, lengths, cotangent, w_query, w_key, w_value, w_out):
    full_query, full_key, full_value, full_out = (
        lax.all_gather(w_query, "dp", axis=0, tiled=True),
        lax.all_gather(w_key, "dp", axis=0, tiled=True),
        lax.all_gather(w_value, "dp", axis=0, tiled=True),
        lax.all_gather(w_out, "dp", axis=0, tiled=True),
    )
    inputs = frames[0]
    upstream = cotangent[0]
    length = lengths[0]
    row_count = inputs.shape[0]
    inner_width = full_query.shape[1]
    head_count = inner_width // HEAD
    score_scale = HEAD ** (-0.5)
    first_frame = lax.axis_index("ctx") * row_count
    row_usable = first_frame + jnp.arange(row_count) < length
    queries = jnp.dot(inputs, full_query, preferred_element_type=jnp.float32).astype(jnp.bfloat16)
    keys = jnp.dot(inputs, full_key, preferred_element_type=jnp.float32).astype(jnp.bfloat16)
    values = jnp.dot(inputs, full_value, preferred_element_type=jnp.float32).astype(jnp.bfloat16)
    query_heads = head_split(queries, head_count)
    key_heads = head_split(keys, head_count)
    value_heads = head_split(values, head_count)
    start_state = (
        jnp.full((head_count, row_count), MASKED_SCORE, jnp.float32),
        jnp.zeros((head_count, row_count), jnp.float32),
        jnp.zeros((head_count, row_count, HEAD), jnp.float32),
    )
    all_keys, all_values = (
        lax.all_gather(keys, "ctx", axis=0, tiled=True),
        lax.all_gather(values, "ctx", axis=0, tiled=True),
    )
    key_block = row_count * math.gcd(max(1, 512 // row_count), lax.axis_size("ctx"))
    block_count = all_keys.shape[0] // key_block
    key_blocks = all_keys.reshape(block_count, key_block, inner_width)
    value_blocks = all_values.reshape(block_count, key_block, inner_width)
    block_starts = jnp.arange(block_count, dtype=jnp.int32) * key_block

    def scan_forward(current, scan_item):
        return (
            forward_step(
                current, scan_item[0], scan_item[1], scan_item[2], query_heads, length, score_scale
            ),
            None,
        )

    softmax_state, unused = lax.scan(
        scan_forward, start_state, (key_blocks, value_blocks, block_starts)
    )
    maxima, totals, accumulated = softmax_state
    context = (
        (accumulated / totals[:, :, None])
        .transpose(1, 0, 2)
        .reshape(row_count, inner_width)
        .astype(jnp.bfloat16)
    )
    logsum = maxima + jnp.log(totals)
    attended = jnp.dot(context, full_out, preferred_element_type=jnp.float32)
    attended = jnp.where(row_usable[:, None], attended, 0.0).astype(jnp.bfloat16)
    masked_grad = jnp.where(row_usable[:, None], upstream, jnp.zeros_like(upstream))
    grad_context = back_project(masked_grad, full_out).astype(jnp.bfloat16)
    deltas = jnp.sum(
        (grad_context.astype(jnp.float32) * context.astype(jnp.float32)).reshape(
            row_count, head_count, HEAD
        ),
        axis=2,
    )
    context_heads = head_split(grad_context, head_count)
    delta_heads = deltas.T
    all_logsum, all_deltas = (
        lax.all_gather(logsum, "ctx", axis=1, tiled=True),
        lax.all_gather(delta_heads, "ctx", axis=1, tiled=True),
    )
    zero_grad = jnp.zeros((row_count, head_count, HEAD), jnp.float32)

    def scan_query(current, scan_item):
        return (
            query_step(
                current,
                scan_item[0],
                scan_item[1],
                scan_item[2],
                query_heads,
                context_heads,
                logsum,
                delta_heads,
                length,
                score_scale,
            ),
            None,
        )

    grad_query, unused = lax.scan(scan_query, zero_grad, (key_blocks, value_blocks, block_starts))
    grad_key, grad_value = key_step(
        lax.all_gather(queries, "ctx", axis=0, tiled=True),
        lax.all_gather(grad_context, "ctx", axis=0, tiled=True),
        all_logsum,
        all_deltas,
        key_heads,
        value_heads,
        row_usable,
        score_scale,
    )
    grad_query = grad_query.reshape(row_count, inner_width).astype(jnp.bfloat16)
    grad_key = grad_key.reshape(row_count, inner_width).astype(jnp.bfloat16)
    grad_value = grad_value.reshape(row_count, inner_width).astype(jnp.bfloat16)
    grad_input = (
        back_project(grad_query, full_query)
        + back_project(grad_key, full_key)
        + back_project(grad_value, full_value)
    )
    grad_frames = grad_input.astype(jnp.bfloat16)
    summed_grad = lax.psum(
        lax.dot_general(
            context, masked_grad, (((0,), (0,)), ((), ())), preferred_element_type=jnp.float32
        ),
        ("rep", "ctx"),
    )
    grad_out = lax.psum_scatter(summed_grad, "dp", scatter_dimension=0, tiled=True)
    return (attended[None], grad_frames[None], grad_out)


MESH = pl.DeviceIdType.MESH


def dot(left, right, left_dim, right_dim):
    return lax.dot_general(
        left, right, (((left_dim,), (right_dim,)), ((), ())), preferred_element_type=jnp.float32
    )


def fused_kernel(
    frames_ref,
    length_ref,
    cot_ref,
    wq_ref,
    wk_ref,
    wv_ref,
    wo_ref,
    attended_ref,
    grad_frames_ref,
    grad_out_ref,
    xs,
    upstream,
    mine,
    cs,
    wq,
    wk,
    wv,
    wo,
    qs,
    ks,
    vs,
    gs,
    ctx,
    logsum,
    deltas,
    dq,
    dk,
    dv,
    part,
    part_in,
    slices,
    send_sem,
    recv_sem,
    local_sem,
):
    rep, dp, z = lax.axis_index("rep"), lax.axis_index("dp"), lax.axis_index("ctx")
    count = 4
    heads = 4
    rows = frames_ref.shape[1]
    full = rows * count
    width = slices.shape[2]
    scale = HEAD ** (-0.5)
    sibling = dp + 1 - 2 * lax.rem(dp, 2)
    across = lax.rem(dp + 2, 4)
    across_sibling = lax.rem(sibling + 2, 4)
    other_rep = 1 - rep
    group = rep * 4 + dp

    local = [
        pltpu.make_async_copy(source, target, local_sem.at[at])
        for at, (source, target) in enumerate(
            (
                (wk_ref, wk.at[dp]),
                (wv_ref, wv.at[dp]),
                (wq_ref, wq.at[dp]),
                (wo_ref, wo.at[dp]),
                (frames_ref.at[0], xs.at[z]),
                (cot_ref.at[0], upstream),
            )
        )
    ]
    for copy in local:
        copy.start()

    barrier = pltpu.get_barrier_semaphore()
    for step in range(1, count):
        pl.semaphore_signal(
            barrier, inc=1, device_id=(rep, dp, lax.rem(z + step, count)), device_id_type=MESH
        )
    for step in range(1, 8):
        peer = lax.rem(group + step, 8)
        pl.semaphore_signal(
            barrier, inc=1, device_id=(peer // 4, lax.rem(peer, 4), z), device_id_type=MESH
        )
    pl.semaphore_wait(barrier, 10)

    def remote(source, target, index, device):
        return pltpu.make_async_remote_copy(
            src_ref=source,
            dst_ref=target,
            send_sem=send_sem.at[index],
            recv_sem=recv_sem.at[index],
            device_id=device,
            device_id_type=MESH,
        )

    def chain(which, side, hop):
        sign = 1 - 2 * side
        pool = (xs, gs)[which]
        owner = z - sign * (hop - 1)
        slot = jnp.clip(owner, 0, count - 1)
        source = frames_ref.at[0] if which == 0 and hop == 1 else pool.at[slot]
        target = jnp.clip(z + sign, 0, count - 1)
        index = which * 6 + side * 3 + hop - 1
        valid = (z + sign >= 0) & (z + sign < count) & (owner >= 0) & (owner < count)
        return valid, remote(source, pool.at[slot], index, (rep, dp, target))

    def chain_send(which, hop):
        for side in range(2):
            valid, copy = chain(which, side, hop)

            @pl.when(valid)
            def _():
                copy.start()

    def chain_recv(which, hop):
        for side in range(2):
            sign = 1 - 2 * side
            pool = (xs, gs)[which]
            owner = z - sign * hop
            slot = jnp.clip(owner, 0, count - 1)
            index = which * 6 + side * 3 + hop - 1

            @pl.when((owner >= 0) & (owner < count))
            def _():
                remote(pool.at[slot], pool.at[slot], index, (rep, dp, z)).wait_recv()

    weights = ((wo_ref, wo), (wk_ref, wk), (wv_ref, wv), (wq_ref, wq))

    def half(ref, which):
        size = ref.shape[0] // 2
        return ref.at[pl.ds(pl.multiple_of(which * size, size), size)]

    def chunk(ref, which, at):
        size = ref.shape[0] // 4
        return ref.at[pl.ds(pl.multiple_of((which * 2 + at) * size, size), size)]

    def weight_copy(piece, step):
        shard, pool = weights[piece]
        index = 12 + piece * 7 + step
        if step == 0:
            return remote(shard, pool.at[dp], index, (rep, sibling, z))
        if step < 3:
            target = chunk(pool.at[dp], rep, step - 1)
            return remote(chunk(shard, rep, step - 1), target, index, (rep, across, z))
        mine_at = pool.at[across]
        if step < 5:
            source = chunk(mine_at, rep, step - 3)
            return remote(source, source, index, (other_rep, dp, z))
        source = half(mine_at, rep if step == 5 else other_rep)
        return remote(source, source, index, (rep, sibling, z))

    def weight_recv(piece, step):
        pool = weights[piece][1]
        index = 12 + piece * 7 + step
        if step == 0:
            target = pool.at[sibling]
        elif step < 3:
            target = chunk(pool.at[across], rep, step - 1)
        elif step < 5:
            target = chunk(pool.at[across], other_rep, step - 3)
        else:
            target = half(pool.at[across_sibling], rep if step == 5 else other_rep)
        remote(target, target, index, (rep, dp, z)).wait_recv()

    def finish_chunk(at):
        weight_recv(at // 2, 3 + at % 2)
        if at % 2 == 1:
            weight_copy(at // 2, 6).start()

    def weight_chunk(at):
        weight_recv(at // 2, 1 + at % 2)
        weight_copy(at // 2, 3 + at % 2).start()
        if at + 2 < 8:
            weight_copy((at + 2) // 2, 1 + at % 2).start()
        if at % 2 == 1:
            weight_copy(at // 2, 5).start()
        if at >= 2:
            finish_chunk(at - 2)

    def cot_copy(step):
        peer = lax.rem(z + step, count)
        return remote(mine.at[peer], cs.at[z], 52 + step, (rep, dp, peer))

    chain_send(0, 1)
    for at in range(2):
        weight_copy(0, 1 + at).start()
    for piece in range(4):
        weight_copy(piece, 0).start()
    for copy in local:
        copy.wait()

    length = length_ref[0]
    columns = [slice(at * width, (at + 1) * width) for at in range(count)]
    real = z * rows + lax.broadcasted_iota(jnp.int32, (rows, width), 0) < length
    for at in range(count):
        kept = jnp.where(real, upstream[:, columns[at]].astype(jnp.float32), 0.0)
        mine[at] = kept.astype(jnp.bfloat16)
    cs[z] = mine[z]

    for at in range(4):
        weight_chunk(at)
    chain_recv(0, 1)
    chain_send(0, 2)
    for at in range(4, 6):
        weight_chunk(at)
    for step in (0, 5, 6):
        weight_recv(0, step)
    masked = jnp.concatenate([mine[at] for at in range(count)], axis=1)
    matrix = dot(masked, wo[...].reshape(512, 1024), 1, 1).astype(jnp.bfloat16)
    for head in range(heads):
        gs[z, head] = matrix[:, head * HEAD : (head + 1) * HEAD]
    weight_chunk(6)
    chain_recv(0, 2)
    chain_send(0, 3)
    for step in range(1, count):
        cot_copy(step).start()
    chain_send(1, 1)
    weight_chunk(7)
    finish_chunk(6)
    finish_chunk(7)
    for piece in range(1, 4):
        for step in (0, 5, 6):
            weight_recv(piece, step)

    def project(block):
        inputs = xs[block]
        start = pl.multiple_of(block * rows, rows)
        for pool, kept in ((wk, ks), (wv, vs), (wq, qs)):
            matrix = dot(inputs, pool[...].reshape(1024, 512), 1, 0).astype(jnp.bfloat16)
            for head in range(heads):
                kept[head, pl.ds(start, rows), :] = matrix[:, head * HEAD : (head + 1) * HEAD]

    def project_hops(first, last):
        def body(step, carry):
            hop = step // 2
            block = z + hop * (1 - 2 * lax.rem(step, 2))

            @pl.when((block >= 0) & (block < count))
            def _():
                project(jnp.clip(block, 0, count - 1))

            return carry

        lax.fori_loop(first, last, body, 0)

    project_hops(1, 6)
    chain_recv(0, 3)
    project_hops(6, 8)

    def key_mask(amount):
        return lax.broadcasted_iota(jnp.int32, (amount, full), 1) < length

    def forward(step, carry):
        head = step // 2
        amount = full // 2
        start = pl.multiple_of(lax.rem(step, 2) * amount, amount)
        usable = key_mask(amount)
        scores = dot(qs[head, pl.ds(start, amount), :], ks[head], 1, 1) * scale
        scores = jnp.where(usable, scores, MASKED_SCORE)
        maxima = jnp.max(scores, axis=1, keepdims=True)
        exponent = jnp.exp(scores - maxima)
        totals = jnp.sum(exponent, axis=1, keepdims=True)
        mixed = dot(exponent.astype(jnp.bfloat16), vs[head], 1, 0)
        ctx[head, pl.ds(start, amount), :] = (mixed * (1.0 / totals)).astype(jnp.bfloat16)
        logsum[head, pl.ds(start, amount), :] = maxima + jnp.log(totals)
        return carry

    lax.fori_loop(0, 4, forward, 0)
    chain_recv(1, 1)
    chain_send(1, 2)
    lax.fori_loop(4, 8, forward, 0)

    own = pl.ds(pl.multiple_of(z * rows, rows), rows)
    for step in range(1, count):
        source = lax.rem(z + count - step, count)
        remote(cs.at[source], cs.at[source], 52 + step, (rep, dp, z)).wait_recv()
    masked_slice = cs[...].reshape(full, width)
    for head in range(heads):
        part[head] = dot(ctx[head], masked_slice, 0, 0).astype(jnp.bfloat16)

    def part_copy(step):
        peer = lax.rem(group + step, 8)
        peer_dp = lax.rem(peer, 4)
        return remote(part.at[peer_dp], part_in.at[step], 40 + step, (peer // 4, peer_dp, z))

    for step in range(1, 8):
        part_copy(step).start()
    chain_recv(1, 2)
    chain_send(1, 3)

    own_context = jnp.concatenate([ctx[head, own, :] for head in range(heads)], axis=1)
    attended = dot(own_context, wo[...].reshape(512, 1024), 1, 0)
    row_at = z * rows + lax.broadcasted_iota(jnp.int32, attended.shape, 0)
    attended_ref[0] = jnp.where(row_at < length, attended, 0.0).astype(jnp.bfloat16)

    total = part[dp].astype(jnp.float32)
    for step in range(1, 8):
        part_copy(step).wait_recv()
        total = total + part_in[step].astype(jnp.float32)
    slices[z] = total.astype(jnp.bfloat16)

    def slice_copy(step):
        return remote(
            slices.at[z], slices.at[z], 48 + step, (rep, dp, lax.rem(z + step, count))
        )

    for step in range(1, count):
        slice_copy(step).start()

    chain_recv(1, 3)

    def backward(head, carry):
        queries, keys, values = qs[head], ks[head], vs[head]
        grads = gs[:, head].reshape(full, HEAD)
        terms = grads.astype(jnp.float32) * ctx[head].astype(jnp.float32)
        deltas[...] = jnp.sum(terms, axis=1, keepdims=True)
        own_keys, own_values = ks[head, own, :], vs[head, own, :]
        scores = dot(queries, own_keys, 1, 1) * scale
        at = z * rows + lax.broadcasted_iota(jnp.int32, scores.shape, 1)
        attention = jnp.where(at < length, jnp.exp(scores - logsum[head]), 0.0)
        dv[head] = dot(attention.astype(jnp.bfloat16), grads, 0, 0).astype(jnp.bfloat16)
        grad_prob = dot(grads, own_values, 1, 1)
        grad_score = (attention * (grad_prob - deltas[...])).astype(jnp.bfloat16)
        dk[head] = (dot(grad_score, queries, 0, 0) * scale).astype(jnp.bfloat16)
        scores = dot(qs[head, own, :], keys, 1, 1) * scale
        attention = jnp.where(key_mask(rows), jnp.exp(scores - logsum[head, own, :]), 0.0)
        grad_prob = dot(gs[z, head], values, 1, 1)
        grad_score = (attention * (grad_prob - deltas[own, :])).astype(jnp.bfloat16)
        dq[head] = (dot(grad_score, keys, 1, 0) * scale).astype(jnp.bfloat16)
        return carry

    lax.fori_loop(0, heads, backward, 0)

    grads = [
        jnp.concatenate([kept[head] for head in range(heads)], axis=1) for kept in (dq, dk, dv)
    ]
    for shard in range(4):
        added = (
            dot(grads[0], wq[shard], 1, 1)
            + dot(grads[1], wk[shard], 1, 1)
            + dot(grads[2], wv[shard], 1, 1)
        )
        grad_frames_ref[0, :, shard * 256 : (shard + 1) * 256] = added.astype(jnp.bfloat16)

    for piece in range(4):
        for step in range(7):
            weight_copy(piece, step).wait_send()
    for which in range(2):
        for hop in range(1, count):
            for side in range(2):
                valid, copy = chain(which, side, hop)

                @pl.when(valid)
                def _():
                    copy.wait_send()

    for step in range(1, count):
        cot_copy(step).wait_send()
    for step in range(1, 8):
        part_copy(step).wait_send()
    for step in range(1, count):
        source = lax.rem(z + count - step, count)
        remote(slices.at[source], slices.at[source], 48 + step, (rep, dp, z)).wait_recv()
    for step in range(1, count):
        slice_copy(step).wait_send()
    for at in range(count):
        grad_out_ref[:, at * width : (at + 1) * width] = slices[at].astype(jnp.float32)


def fused(frames, lengths, cotangent, w_query, w_key, w_value, w_out):
    vmem = pl.BlockSpec(memory_space=pltpu.VMEM)
    hbm = pl.BlockSpec(memory_space=pltpu.HBM)
    bf16, f32 = jnp.bfloat16, jnp.float32
    per_head = pltpu.VMEM((4, 512, HEAD), bf16)
    own_head = pltpu.VMEM((4, 128, HEAD), bf16)
    return pl.pallas_call(
        fused_kernel,
        out_shape=(
            jax.ShapeDtypeStruct(frames.shape, bf16),
            jax.ShapeDtypeStruct(frames.shape, bf16),
            jax.ShapeDtypeStruct(w_out.shape, f32),
        ),
        in_specs=[hbm, pl.BlockSpec(memory_space=pltpu.SMEM)] + [hbm] * 5,
        out_specs=(vmem, vmem, vmem),
        scratch_shapes=[
            pltpu.VMEM((4, 128, 1024), bf16),
            pltpu.VMEM((128, 1024), bf16),
            pltpu.VMEM((4, 128, 256), bf16),
            pltpu.VMEM((4, 128, 256), bf16),
            pltpu.VMEM((4, 256, 512), bf16),
            pltpu.VMEM((4, 256, 512), bf16),
            pltpu.VMEM((4, 256, 512), bf16),
            pltpu.VMEM((4, 128, 1024), bf16),
            per_head,
            per_head,
            per_head,
            pltpu.VMEM((4, 4, 128, HEAD), bf16),
            per_head,
            pltpu.VMEM((4, 512, 1), f32),
            pltpu.VMEM((512, 1), f32),
            own_head,
            own_head,
            own_head,
            pltpu.VMEM((4, 128, 256), bf16),
            pltpu.VMEM((8, 128, 256), bf16),
            pltpu.VMEM((4, 128, 256), bf16),
            pltpu.SemaphoreType.DMA((56,)),
            pltpu.SemaphoreType.DMA((56,)),
            pltpu.SemaphoreType.DMA((6,)),
        ],
        compiler_params=pltpu.CompilerParams(
            collective_id=0, has_side_effects=True, vmem_limit_bytes=48 * 1024 * 1024
        ),
    )(frames, lengths, cotangent, w_query, w_key, w_value, w_out)


def either(sizes, frames, lengths, cotangent, w_query, w_key, w_value, w_out):
    fits = sizes == (2, 4, 4) and frames.shape == (1, 128, 1024) and w_query.shape == (256, 512)
    chosen = fused if fits else shards
    return chosen(frames, lengths, cotangent, w_query, w_key, w_value, w_out)


def solution(mesh):
    in_specs = (
        P(("rep", "dp"), "ctx", None),
        P(("rep", "dp")),
        P(("rep", "dp"), "ctx", None),
        P("dp", None),
        P("dp", None),
        P("dp", None),
        P("dp", None),
    )
    out_specs = (P(("rep", "dp"), "ctx", None), P(("rep", "dp"), "ctx", None), P("dp", None))
    sizes = (mesh.shape["rep"], mesh.shape["dp"], mesh.shape["ctx"])
    body = functools.partial(either, sizes)
    return jax.shard_map(body, mesh=mesh, in_specs=in_specs, out_specs=out_specs, check_vma=False)
```
